32 devices in a mesh: row: 8 (over z, y), col: 4 (over x, core).
Axes of the slice: x: 2, y: 2, z: 4, core: 2. Of those that a mesh axis runs over, the one named last changes fastest.
Arguments:
- left_blocks: float32 [8, 8, 4, 4096], P('row', 'col'), may hold values from -0.75 to 0.75
- right_blocks: float32 [8, 4, 20, 4096], P('row', 'col'), may hold values from -6 to 6
- left_slots: int32 [8, 4, 4, 2, 24], P('row', 'col'), may hold values from 0 to 3
- right_slots: int32 [8, 4, 4, 2, 24], P('row', 'col'), may hold values from 0 to 19
- sink_slots: int32 [8, 4, 4, 2, 24], P('row', 'col'), may hold values from 0 to 11
- live_counts: int32 [8, 4, 4, 2], P('row', 'col'), may hold values from 3 to 24, as said below
Outputs:
- product_blocks: float32 [8, 4, 12, 4096], P('row', 'col')
The draws below stay inside these ranges and needn't reach their ends.
Inputs may be any that keep to these rules, and one draw needn't show every extreme that they name: `live_counts`: entries of a list at positions from its live count on are not read; at least one list in every draw is full.
All inputs are finite; a program needn't handle non-finite values.
Results may differ from the reference program's by a relative error of at most 0.0003.
Values sent between devices are 32-bit elements; how exact they have to be, the bound alone decides.
No kernel may reach another device: no remote copies, remote signals or barrier semaphores. Data moves between devices by JAX's collectives and lax.ppermute only.
A program may use at most 64 MiB of HBM per device.

```python
import jax
import jax.numpy as jnp
from jax import lax

TILE_SIDE = 64
LEFT_SLOTS = 4
RIGHT_SLOTS = 20
SINK_SLOTS = 12
PRODUCTS = 24
SECTIONS = 4
INNER_PANELS = 8
N_ROW = 8
N_COL = 4


def draw_live_counts(key, part):
    shape = (N_ROW, N_COL, SECTIONS, 2)
    first_key, second_key, third_key = jax.random.split(key, 3)
    base_counts = jax.random.randint(first_key, shape, PRODUCTS // 8, PRODUCTS // 2 + 1)
    full_lists = jax.random.randint(second_key, shape, 0, 8) == 0
    chosen = jax.random.randint(third_key, (), 0, N_ROW * N_COL * SECTIONS * 2)
    position = jnp.arange(N_ROW * N_COL * SECTIONS * 2).reshape(shape)
    counts = jnp.where(full_lists | (position == chosen), PRODUCTS, base_counts)
    return counts.astype(jnp.int32)


def touch_ends(values, key, least, largest):
    longest = values.shape.index(max(values.shape))
    spots = []
    for shift in (0, 1):
        where = [jax.random.randint(jax.random.fold_in(key, axis), (), 0, length) for axis, length in enumerate(values.shape)]
        where[longest] = (where[longest] + shift) % values.shape[longest]
        spots.append(tuple(where))
    return values.at[spots[0]].set(least).at[spots[1]].set(largest)


def steps_of(own_key, shape, shards, least, top_value):
    gain = 1.0
    for dim, blocks in shards:
        steps = jax.random.uniform(jax.random.fold_in(jax.random.fold_in(own_key, 6), dim), (blocks,), jnp.float32, least / len(shards), top_value / len(shards))
        gain = gain * jnp.repeat(jnp.exp(steps), shape[dim] // blocks).reshape((-1,) + (1,) * (len(shape) - 1 - dim))
    return gain


def noise(stream_key, extent, deviation, limit, cuts=(), held_as=jnp.bfloat16):
    gain = steps_of(stream_key, extent, cuts, -0.22, 0.18) if cuts else 1.0
    drawn = jax.random.normal(stream_key, extent, jnp.float32) * deviation * gain
    return jnp.minimum(jnp.maximum(drawn, -limit), limit).astype(held_as)


def setup_inputs(seed: int = 0) -> dict:
    seeds = jax.random.split(jax.random.key(seed), 7)
    return {
        "left_blocks": noise(seeds[0], (N_ROW, INNER_PANELS, LEFT_SLOTS, TILE_SIDE * TILE_SIDE), TILE_SIDE ** -0.5, 0.75, ((0, 8), (1, 4)), jnp.float32),
        "right_blocks": noise(seeds[1], (INNER_PANELS, N_COL, RIGHT_SLOTS, TILE_SIDE * TILE_SIDE), 1.0, 6.0, ((0, 8), (1, 4)), jnp.float32),
        "left_slots": touch_ends(jax.random.randint(seeds[2], (N_ROW, N_COL, SECTIONS, 2, PRODUCTS), 0, LEFT_SLOTS), jax.random.fold_in(seeds[2], 1), 0, LEFT_SLOTS - 1).astype(jnp.int32),
        "right_slots": touch_ends(jax.random.randint(seeds[3], (N_ROW, N_COL, SECTIONS, 2, PRODUCTS), 0, RIGHT_SLOTS), jax.random.fold_in(seeds[3], 1), 0, RIGHT_SLOTS - 1).astype(jnp.int32),
        "sink_slots": touch_ends(jax.random.randint(seeds[4], (N_ROW, N_COL, SECTIONS, 2, PRODUCTS), 0, SINK_SLOTS), jax.random.fold_in(seeds[4], 1), 0, SINK_SLOTS - 1).astype(jnp.int32),
        "live_counts": draw_live_counts(jax.random.fold_in(seeds[6], 71), 0),
    }


def block_terms(left_panel, right_panel, left_index, right_index, sink_index, live_count):
    is_live = (jnp.arange(PRODUCTS) < live_count).astype(jnp.float32)
    left_tiles = jnp.take(left_panel, left_index, axis=0).reshape(PRODUCTS, TILE_SIDE, TILE_SIDE)
    right_tiles = jnp.take(right_panel, right_index, axis=0).reshape(PRODUCTS, TILE_SIDE, TILE_SIDE)
    products = jnp.einsum("pik,pkj->pij", left_tiles.astype(jnp.float32), right_tiles.astype(jnp.float32), precision=lax.Precision.HIGHEST)
    products = products.reshape(PRODUCTS, TILE_SIDE * TILE_SIDE) * is_live[:, None]
    return jax.ops.segment_sum(products, sink_index, num_segments=SINK_SLOTS)


def reference(left_blocks, right_blocks, left_slots, right_slots, sink_slots, live_counts):
    def one_panel(flat_index):
        row_no = flat_index // N_COL
        col_no = flat_index % N_COL
        left_row = lax.dynamic_index_in_dim(left_blocks, row_no, 0, keepdims=False)
        right_col = lax.dynamic_index_in_dim(right_blocks, col_no, 1, keepdims=False)
        running = jnp.zeros((SINK_SLOTS, TILE_SIDE * TILE_SIDE), jnp.float32)
        for section_no in range(SECTIONS):
            for half_no in range(2):
                inner = (2 * ((row_no // 2 + col_no + section_no) % N_COL) + half_no).astype(jnp.int32)
                left_panel = lax.dynamic_index_in_dim(left_row, inner, 0, keepdims=False)
                right_panel = lax.dynamic_index_in_dim(right_col, inner, 0, keepdims=False)
                running = running + block_terms(left_panel, right_panel,
                                                left_slots[row_no, col_no, section_no, half_no],
                                                right_slots[row_no, col_no, section_no, half_no],
                                                sink_slots[row_no, col_no, section_no, half_no],
                                                live_counts[row_no, col_no, section_no, half_no])
        return running

    result = lax.map(one_panel, jnp.arange(N_ROW * N_COL, dtype=jnp.int32))
    return result.reshape(N_ROW, N_COL, SINK_SLOTS, TILE_SIDE * TILE_SIDE)
```

```python
import functools

import jax
import jax.numpy as jnp
from jax import lax
from jax.experimental import pallas as pl
from jax.experimental.pallas import tpu as pltpu
from jax.sharding import PartitionSpec as P

TILE_SIDE = 64
LEFT_SLOTS = 4
RIGHT_SLOTS = 20
SINK_SLOTS = 12
PRODUCTS = 24
SECTIONS = 4
HALF = TILE_SIDE // 2
LANES = 2 * TILE_SIDE
AXES = ("row", "col")
MIB = 1 << 20


def in_low_half(shape):
    return lax.broadcasted_iota(jnp.int32, shape, 1) % LANES < TILE_SIDE


def spread_table():
    shape = (2 * LANES, 8 * TILE_SIDE)
    source = lax.broadcasted_iota(jnp.int32, shape, 0)
    target = lax.broadcasted_iota(jnp.int32, shape, 1)
    place = target % TILE_SIDE
    part = target // TILE_SIDE % 2
    odd_row = target // (4 * TILE_SIDE)
    inner = 2 * (place % HALF) + place // HALF
    return (source == part * LANES + odd_row * TILE_SIDE + inner).astype(jnp.bfloat16)


def spread_left(blocks, table):
    high = blocks.astype(jnp.bfloat16)
    low = (blocks - high.astype(jnp.float32)).astype(jnp.bfloat16)
    both = jnp.concatenate([high, low], axis=1)
    wide = jnp.dot(both, table, preferred_element_type=jnp.float32).astype(jnp.bfloat16)
    return jnp.concatenate([wide[:, : 4 * TILE_SIDE], wide[:, 4 * TILE_SIDE :]], axis=0)


def slots_in_order(panel_ref, half):
    return jnp.concatenate(
        [panel_ref[half, pl.ds(slot, HALF, stride=LEFT_SLOTS), :] for slot in range(LEFT_SLOTS)], axis=0
    )


def right_pair(first, second):
    low_half = in_low_half((HALF, LANES))
    first_turned = pltpu.roll(first, TILE_SIDE, 1)
    second_turned = pltpu.roll(second, TILE_SIDE, 1)
    even = jnp.where(low_half, first, second_turned)
    odd = jnp.where(low_half, first_turned, second)
    rows = jnp.concatenate([even, odd], axis=0)
    high = rows.astype(jnp.bfloat16)
    low = (rows - high.astype(jnp.float32)).astype(jnp.bfloat16)
    return jnp.concatenate([high, high, low, low], axis=0)


def all_products(lefts, right_ref, product_refs):
    rows = LEFT_SLOTS * HALF
    left = lefts[0] if len(lefts) == 1 else jnp.concatenate(lefts, axis=0)
    low_half = in_low_half((HALF, LANES))
    for slot in range(0, RIGHT_SLOTS, 4):
        weights = jnp.concatenate(
            [right_pair(right_ref[slot + n], right_ref[slot + n + 1]) for n in (0, 2)], axis=1
        )
        result = jnp.dot(left, weights, preferred_element_type=jnp.float32)
        for t, product_ref in enumerate(product_refs):
            for l in range(LEFT_SLOTS):
                for n in (0, 2):
                    start = t * 2 * rows + l * HALF
                    even = result[start : start + HALF, n * TILE_SIDE : (n + 2) * TILE_SIDE]
                    odd = result[start + rows : start + rows + HALF, n * TILE_SIDE : (n + 2) * TILE_SIDE]
                    place = l * RIGHT_SLOTS + slot + n
                    product_ref[place] = jnp.where(low_half, even, pltpu.roll(odd, TILE_SIDE, 1))
                    product_ref[place + 1] = jnp.where(low_half, pltpu.roll(even, TILE_SIDE, 1), odd)


def add_listed(total_ref, product_ref, lists, section, half):
    left_ref, right_ref, sink_ref, count_ref = lists
    live = count_ref[section, half]
    for p in range(PRODUCTS):
        place = left_ref[section, half, p] * RIGHT_SLOTS + right_ref[section, half, p]
        sink = jnp.where(p < live, sink_ref[section, half, p], SINK_SLOTS)
        total_ref[sink] += product_ref[place]


def group_kernel(
    meta, near_l, near_r, near_s, near_n, far_l, far_r, far_s, far_n,
    own, q1, q2, r1, r2, r3, right_own, right_y, right_z,
    near_out, far_out, near_left_d, far_left_d,
    lefts, near_total, far_total, near_products, far_products,
):
    table = spread_table()
    inside = meta[0] == 1
    for half in range(2):
        def pick(a, b, half=half):
            return jnp.where(inside, slots_in_order(a, half), slots_in_order(b, half))
        lefts[0, 0, half] = spread_left(pick(own, q1), table)
        lefts[0, 1, half] = spread_left(pick(q2, r1), table)
        lefts[1, 0, half] = spread_left(pick(q1, r2), table)
        lefts[1, 1, half] = spread_left(pick(r1, r3), table)
    near_total[...] = jnp.zeros_like(near_total)
    far_total[...] = jnp.zeros_like(far_total)
    near_lists = (near_l, near_r, near_s, near_n)
    far_lists = (far_l, far_r, far_s, far_n)
    half = meta[1]
    for right, level, in_half in ((right_own, 0, half), (right_y, 0, 1 - half), (right_z, 1, half)):
        which = meta[2 + level]
        all_products(
            [lefts[0, which, in_half], lefts[1, which, in_half]], right, [near_products, far_products]
        )
        add_listed(far_total, far_products, far_lists, meta[6 + level], in_half)
        add_listed(near_total, near_products, near_lists, meta[4 + level], in_half)
    near_out[...] = near_total[:SINK_SLOTS]
    far_out[...] = far_total[:SINK_SLOTS]
    near_left_d[...] = lefts[0, meta[3], 1 - half]
    far_left_d[...] = lefts[1, meta[3], 1 - half]


def last_kernel(meta, l, r, s, n, left, right, before, out, total, products, *, far):
    total[:SINK_SLOTS] = before[...]
    all_products([left[...]], right, [products])
    add_listed(total, products, (l, r, s, n), meta[7 if far else 5], 1 - meta[1])
    out[...] = total[:SINK_SLOTS]


def pair_kernel(meta, l, r, s, n, left, right_0, right_1, before, out, total, products):
    table = spread_table()
    total[:SINK_SLOTS] = before[...]
    for half, right in ((0, right_0), (1, right_1)):
        all_products([spread_left(slots_in_order(left, half), table)], right, [products])
        add_listed(total, products, (l, r, s, n), meta[0], half)
    out[...] = total[:SINK_SLOTS]


SMEM = pl.BlockSpec(memory_space=pltpu.SMEM)
VMEM = pl.BlockSpec(memory_space=pltpu.VMEM)
SUMS = (SINK_SLOTS, HALF, LANES)
TOTAL = pltpu.VMEM((SINK_SLOTS + 1, HALF, LANES), jnp.float32)
PRODUCT_TABLE = pltpu.VMEM((LEFT_SLOTS * RIGHT_SLOTS, HALF, LANES), jnp.float32)
SPREAD = (2 * LEFT_SLOTS * HALF, 4 * TILE_SIDE)


def call(kernel, n_smem, n_vmem, outs, scratch, flops, name):
    return pl.pallas_call(
        kernel,
        out_shape=outs,
        in_specs=[SMEM] * n_smem + [VMEM] * n_vmem,
        out_specs=jax.tree.map(lambda _: VMEM, outs),
        scratch_shapes=scratch,
        compiler_params=pltpu.CompilerParams(vmem_limit_bytes=24 * MIB),
        cost_estimate=pl.CostEstimate(flops=flops, bytes_accessed=4 * MIB, transcendentals=0),
        name=name,
    )


def sums():
    return jax.ShapeDtypeStruct(SUMS, jnp.float32)


def spread_shape():
    return jax.ShapeDtypeStruct(SPREAD, jnp.bfloat16)


def left_view(panels):
    halves = panels.shape[0]
    return panels.reshape(halves, LEFT_SLOTS, HALF, LANES).transpose(0, 2, 1, 3).reshape(halves, -1, LANES)


def grouped(left, right, lists):
    cols = lax.axis_size("col")

    def device(pair, parity, col):
        return (2 * pair + parity) * cols + col

    def send(value, to):
        where = [
            (device(pair, parity, col), device(*to(pair, parity, col)))
            for pair in range(cols)
            for parity in range(2)
            for col in range(cols)
        ]
        return lax.ppermute(value, AXES, where)

    row, col = lax.axis_index("row"), lax.axis_index("col")
    pair, parity = row // 2, row % 2
    core = col % 2
    inside = (col // 2 == pair // 2).astype(jnp.int32)
    level_0 = (pair % 2 != core).astype(jnp.int32)
    far_pair = pair ^ 2
    meta = jnp.stack(
        [
            inside,
            parity,
            level_0,
            1 - level_0,
            (pair - pair - col) % cols,
            ((pair ^ 1) - pair - col) % cols,
            (pair - far_pair - col) % cols,
            ((pair ^ 1) - far_pair - col) % cols,
        ]
    ).astype(jnp.int32)

    def left_home(pair, parity, col):
        return (pair, parity, col ^ 2) if col // 2 == pair // 2 else (pair ^ 2, parity, col)

    q1 = send(left, left_home)
    right_y = send(right, lambda pair, parity, col: (pair, 1 - parity, col))
    right_z = send(right, lambda pair, parity, col: (pair ^ 1, parity, col))
    right_d = send(right, lambda pair, parity, col: (pair ^ 1, 1 - parity, col))
    q2 = send(left, lambda pair, parity, col: (pair, parity, col ^ 1))
    left_list, right_list, sink_list, counts = lists
    packed = jnp.concatenate([left_list, right_list, sink_list, counts[..., None]], axis=-1)
    packed = send(packed, lambda pair, parity, col: (pair ^ 2, parity, col))
    far_lists = tuple(packed[..., n * PRODUCTS : (n + 1) * PRODUCTS] for n in range(3)) + (packed[..., -1],)
    r1 = send(q1, lambda pair, parity, col: (pair, parity, col ^ 1))
    r2 = send(q1, lambda pair, parity, col: (pair, parity, col ^ 2))
    r3 = send(q1, lambda pair, parity, col: (pair, parity, col ^ 3))

    near, far, near_left, far_left = call(
        group_kernel, 9, 9,
        (sums(), sums(), spread_shape(), spread_shape()),
        [pltpu.VMEM((2, 2, 2) + SPREAD, jnp.bfloat16), TOTAL, TOTAL, PRODUCT_TABLE, PRODUCT_TABLE],
        3 * 10**9, "three_panels",
    )(meta, *lists, *far_lists, left, q1, q2, r1, r2, r3, right, right_y, right_z)
    far = call(
        functools.partial(last_kernel, far=True), 5, 3, sums(), [TOTAL, PRODUCT_TABLE], 10**9, "far_panel"
    )(meta, *far_lists, far_left, right_d, far)
    received = send(far, lambda pair, parity, col: (pair ^ 2, parity, col))
    near = call(
        functools.partial(last_kernel, far=False), 5, 3, sums(), [TOTAL, PRODUCT_TABLE], 10**9, "near_panel"
    )(meta, *lists, near_left, right_d, near)
    return near + received


def shifted(shard, axis, by):
    devices = lax.axis_size(axis)
    return lax.ppermute(shard, axis, [(i, (i + by) % devices) for i in range(devices)])


def windowed(left, right, lists):
    cols = lax.axis_size("col")
    half_row, parity = lax.axis_index("row") // 2, lax.axis_index("row") % 2
    column = lax.axis_index("col")
    bits = cols.bit_length() - 1
    for bit in range(bits):
        right = jnp.where(column // (1 << bit) % 2 == 1, shifted(right, "row", -(2 << bit)), right)
        left = jnp.where(half_row // (1 << bit) % 2 == 1, shifted(left, "col", -(1 << bit)), left)
    total = jnp.zeros(SUMS, jnp.float32)
    for section in range(SECTIONS):
        swap = [(i, i ^ 1) for i in range(lax.axis_size("row"))]
        partner = lax.ppermute(right, "row", swap)
        total = call(pair_kernel, 5, 4, sums(), [TOTAL, PRODUCT_TABLE], 2 * 10**9, "panel_pair")(
            jnp.full((1,), section, jnp.int32), *lists, left,
            jnp.where(parity == 0, right, partner), jnp.where(parity == 0, partner, right), total,
        )
        if section + 1 < SECTIONS:
            right = shifted(right, "row", -2)
            left = shifted(left, "col", -1)
    return total


def per_device(left_blocks, right_blocks, left_slots, right_slots, sink_slots, live_counts):
    left = left_view(left_blocks[0])
    right = right_blocks.reshape(RIGHT_SLOTS, HALF, LANES)
    lists = (left_slots[0, 0], right_slots[0, 0], sink_slots[0, 0], live_counts[0, 0])
    plan = grouped if lax.axis_size("col") == SECTIONS == 4 else windowed
    return plan(left, right, lists).reshape(1, 1, SINK_SLOTS, TILE_SIDE * TILE_SIDE)


def solution(mesh):
    return jax.shard_map(
        per_device,
        mesh=mesh,
        in_specs=(
            P("row", "col", None, None),
            P("row", "col", None, None),
            P("row", "col", None, None, None),
            P("row", "col", None, None, None),
            P("row", "col", None, None, None),
            P("row", "col", None, None),
        ),
        out_specs=P("row", "col", None, None),
        check_vma=False,
    )
```

```python
import functools

import jax
import jax.numpy as jnp
from jax import lax
from jax.experimental import pallas as pl
from jax.experimental.pallas import tpu as pltpu
from jax.sharding import PartitionSpec as P

TILE_SIDE = 64
LEFT_SLOTS = 4
RIGHT_SLOTS = 20
SINK_SLOTS = 12
PRODUCTS = 24
SECTIONS = 4
HALF = TILE_SIDE // 2
LANES = 2 * TILE_SIDE
LEFT_ROWS = 2 * LEFT_SLOTS * HALF
LIST_ROWS = 32
AXES = ("row", "col")
MIB = 1 << 20


def in_low_half(shape):
    return lax.broadcasted_iota(jnp.int32, shape, 1) % LANES < TILE_SIDE


def spread_table():
    shape = (2 * LANES, 8 * TILE_SIDE)
    source = lax.broadcasted_iota(jnp.int32, shape, 0)
    target = lax.broadcasted_iota(jnp.int32, shape, 1)
    place = target % TILE_SIDE
    part = target // TILE_SIDE % 2
    odd_row = target // (4 * TILE_SIDE)
    inner = 2 * (place % HALF) + place // HALF
    return (source == part * LANES + odd_row * TILE_SIDE + inner).astype(jnp.bfloat16)


def spread_left(blocks, table):
    high = blocks.astype(jnp.bfloat16)
    low = (blocks - high.astype(jnp.float32)).astype(jnp.bfloat16)
    both = jnp.concatenate([high, low], axis=1)
    wide = jnp.dot(both, table, preferred_element_type=jnp.float32).astype(jnp.bfloat16)
    return jnp.concatenate([wide[:, : 4 * TILE_SIDE], wide[:, 4 * TILE_SIDE :]], axis=0)


def slots_in_order(panel_ref, half):
    first = half * LEFT_SLOTS * HALF
    return jnp.concatenate(
        [panel_ref[pl.ds(first + slot, HALF, stride=LEFT_SLOTS), :] for slot in range(LEFT_SLOTS)], axis=0
    )


def right_pair(first, second):
    low_half = in_low_half((HALF, LANES))
    first_turned = pltpu.roll(first, TILE_SIDE, 1)
    second_turned = pltpu.roll(second, TILE_SIDE, 1)
    even = jnp.where(low_half, first, second_turned)
    odd = jnp.where(low_half, first_turned, second)
    rows = jnp.concatenate([even, odd], axis=0)
    high = rows.astype(jnp.bfloat16)
    low = (rows - high.astype(jnp.float32)).astype(jnp.bfloat16)
    return jnp.concatenate([high, high, low, low], axis=0)


def all_products(lefts, right_ref, product_refs):
    rows = LEFT_SLOTS * HALF
    left = lefts[0] if len(lefts) == 1 else jnp.concatenate(lefts, axis=0)
    low_half = in_low_half((HALF, LANES))
    for slot in range(0, RIGHT_SLOTS, 4):
        weights = jnp.concatenate(
            [right_pair(right_ref[slot + n], right_ref[slot + n + 1]) for n in (0, 2)], axis=1
        )
        result = jnp.dot(left, weights, preferred_element_type=jnp.float32)
        for t, product_ref in enumerate(product_refs):
            for l in range(LEFT_SLOTS):
                for n in (0, 2):
                    start = t * 2 * rows + l * HALF
                    even = result[start : start + HALF, n * TILE_SIDE : (n + 2) * TILE_SIDE]
                    odd = result[start + rows : start + rows + HALF, n * TILE_SIDE : (n + 2) * TILE_SIDE]
                    place = l * RIGHT_SLOTS + slot + n
                    product_ref[place] = jnp.where(low_half, even, pltpu.roll(odd, TILE_SIDE, 1))
                    product_ref[place + 1] = jnp.where(low_half, pltpu.roll(even, TILE_SIDE, 1), odd)


def add_listed(total_ref, product_ref, lists, section, half):
    for p in range(PRODUCTS):
        product, sink = lists.entry(section, half, p)
        total_ref[sink] += product_ref[product]


class OwnLists:
    def __init__(self, refs):
        self.refs = refs

    def entry(self, section, half, p):
        left, right, sink = (ref[section, half, p] for ref in self.refs[:3])
        live = self.refs[3][section, half]
        return left * RIGHT_SLOTS + right, jnp.where(p < live, sink, SINK_SLOTS)


class SentLists:
    def __init__(self, panel_ref, whole, numbers, semaphore):
        left, right, sink, live = (
            panel_ref[LEFT_ROWS + 8 * n : LEFT_ROWS + 8 * (n + 1), :].astype(jnp.int32) for n in range(4)
        )
        here = lax.broadcasted_iota(jnp.int32, left.shape, 1) < live
        whole[...] = (left * RIGHT_SLOTS + right) * 16 + jnp.where(here, sink, SINK_SLOTS)
        copy = pltpu.make_async_copy(whole, numbers, semaphore)
        copy.start()
        copy.wait()
        self.numbers = numbers

    def entry(self, section, half, p):
        number = self.numbers[section * 2 + half, p]
        return number >> 4, number & 15


class Place:
    def __init__(self):
        self.cols = lax.axis_size("col")
        row, self.col = lax.axis_index("row"), lax.axis_index("col")
        self.pair, self.half = row // 2, row % 2
        self.inside = self.col // 2 == self.pair // 2

    def which_left(self, level):
        return (self.pair + self.col + level) % 2

    def section(self, level, far):
        target = self.pair ^ 3 if far else self.pair
        return ((self.pair ^ level) - target - self.col + 2 * self.cols) % self.cols


def stage_kernel(left, left_list, right_list, sink_list, counts, left_out, rows_out, semaphore):
    copy = pltpu.make_async_copy(left, left_out, semaphore)
    copy.start()
    rows_out[...] = jnp.zeros_like(rows_out)
    for n, ref in enumerate((left_list, right_list, sink_list)):
        for section in range(SECTIONS):
            start = 8 * n + 2 * section
            rows_out[start : start + 2, :PRODUCTS] = ref[section].astype(jnp.float32)
    live = counts[...].astype(jnp.float32)
    for section in range(SECTIONS):
        for half in range(2):
            row = 24 + 2 * section + half
            one = live[section : section + 1, half : half + 1]
            rows_out[row : row + 1, :] = jnp.broadcast_to(one, (1, LANES))
    copy.wait()


def pick_kernel(left, beside, rows, near_out, far_out):
    inside = Place().inside

    @pl.when(inside)
    def _():
        near_out[...] = left[...]
        far_out[:LEFT_ROWS, :] = beside[...]

    @pl.when(jnp.logical_not(inside))
    def _():
        near_out[...] = beside[...]
        far_out[:LEFT_ROWS, :] = left[...]

    far_out[LEFT_ROWS:, :] = rows[...]


def spread_panels(lefts, panels):
    table = spread_table()
    for which, panel in enumerate(panels):
        for half in range(2):
            lefts[which, half] = spread_left(slots_in_order(panel, half), table)


def add_panels(panels, product_ref, total_ref, lists, lefts, place, far):
    for blocks, level, half in panels:
        all_products([lefts[place.which_left(level), half]], blocks, [product_ref])
        add_listed(total_ref, product_ref, lists, place.section(level, far), half)


def far_kernel(
    left_a, left_b, own, right_y, right_z,
    out, left_out, lefts, total, products, whole, numbers, semaphore,
):
    lists = SentLists(left_a, whole, numbers, semaphore)
    place = Place()
    half = place.half
    spread_panels(lefts, (left_a, left_b))
    left_out[...] = lefts[place.which_left(1), 1 - half]
    total[...] = jnp.zeros_like(total)
    panels = ((own, 0, half), (right_y, 0, 1 - half), (right_z, 1, half))
    add_panels(panels, products, total, lists, lefts, place, True)
    out[...] = total[:SINK_SLOTS]


def far_last_kernel(
    left_a, left, right_0, right_1, before, out, total, products, whole, numbers, semaphore
):
    lists = SentLists(left_a, whole, numbers, semaphore)
    place = Place()
    total[:SINK_SLOTS] = before[...]
    all_products([left[...]], Joined(right_0, right_1), [products])
    add_listed(total, products, lists, place.section(1, True), 1 - place.half)
    out[...] = total[:SINK_SLOTS]


def near_kernel(
    l, r, s, n, left_a, left_b, own, right_y, right_z, right_0, right_1, out, lefts, total, products
):
    place = Place()
    half = place.half
    spread_panels(lefts, (left_a, left_b))
    total[...] = jnp.zeros_like(total)
    panels = (
        (own, 0, half), (right_y, 0, 1 - half), (right_z, 1, half), (Joined(right_0, right_1), 1, 1 - half),
    )
    add_panels(panels, products, total, OwnLists((l, r, s, n)), lefts, place, False)
    out[...] = total[:SINK_SLOTS]


class Joined:
    def __init__(self, first, second):
        self.first, self.second = first, second

    def __getitem__(self, index):
        size = self.first.shape[0]
        return self.first[index] if index < size else self.second[index - size]


def pair_kernel(l, r, s, n, left, right_0, right_1, before, out, total, products, *, section):
    table = spread_table()
    total[:SINK_SLOTS] = before[...]
    for half, right in ((0, right_0), (1, right_1)):
        all_products([spread_left(slots_in_order(left, half), table)], right, [products])
        add_listed(total, products, OwnLists((l, r, s, n)), section, half)
    out[...] = total[:SINK_SLOTS]


STAGE_COST = 2 * 10**9
PICK_COST = 0
ANY = pl.BlockSpec(memory_space=pl.ANY)
SMEM = pl.BlockSpec(memory_space=pltpu.SMEM)
VMEM = pl.BlockSpec(memory_space=pltpu.VMEM)
SUMS = (SINK_SLOTS, HALF, LANES)
TOTAL = pltpu.VMEM((SINK_SLOTS + 1, HALF, LANES), jnp.float32)
PRODUCT_TABLE = pltpu.VMEM((LEFT_SLOTS * RIGHT_SLOTS, HALF, LANES), jnp.float32)
SPREAD = (2 * LEFT_SLOTS * HALF, 4 * TILE_SIDE)


def call(kernel, specs, outs, scratch, flops, name):
    return pl.pallas_call(
        kernel,
        out_shape=outs,
        in_specs=specs,
        out_specs=jax.tree.map(lambda _: VMEM, outs),
        scratch_shapes=scratch,
        compiler_params=pltpu.CompilerParams(vmem_limit_bytes=24 * MIB),
        cost_estimate=pl.CostEstimate(flops=flops, bytes_accessed=4 * MIB, transcendentals=0),
        name=name,
    )


def sums():
    return jax.ShapeDtypeStruct(SUMS, jnp.float32)


def left_panel(more):
    return jax.ShapeDtypeStruct((LEFT_ROWS + more, LANES), jnp.float32)


def spread_shape():
    return jax.ShapeDtypeStruct(SPREAD, jnp.bfloat16)


def left_view(panels):
    return panels.reshape(2, LEFT_SLOTS, HALF, LANES).transpose(0, 2, 1, 3).reshape(LEFT_ROWS, LANES)


def grouped(left, right, lists):
    cols = lax.axis_size("col")

    def device(pair, parity, col):
        return (2 * pair + parity) * cols + col

    def send(value, to):
        where = [
            (device(pair, parity, col), device(*to(pair, parity, col)))
            for pair in range(cols)
            for parity in range(2)
            for col in range(cols)
        ]
        return lax.ppermute(value, AXES, where)

    def y_next(pair, parity, col):
        return (pair, 1 - parity, col)

    def z_next(pair, parity, col):
        return (pair ^ 1, parity, col)

    def z_far(pair, parity, col):
        return (pair ^ 3, parity, col)

    def col_next(flip):
        return lambda pair, parity, col: (pair, parity, col ^ flip)

    beside = send(left, col_next(2))
    right_y = send(right, y_next)
    right_z = send(right, z_next)
    own_left, list_rows = call(
        stage_kernel, [ANY] + [VMEM] * 4, (left_panel(0), jax.ShapeDtypeStruct((LIST_ROWS, LANES), jnp.float32)),
        [pltpu.SemaphoreType.DMA(())], STAGE_COST, "stage",
    )(left, *lists)
    near_a, far_a = call(
        pick_kernel, [VMEM] * 3, (left_panel(0), left_panel(LIST_ROWS)), [], PICK_COST, "pick"
    )(own_left, beside, list_rows)
    far_a = send(far_a, z_far)
    cut = RIGHT_SLOTS // 2
    right_0 = send(right_z[:cut], y_next)
    right_1 = send(right_y[cut:], z_next)
    far_b = send(far_a, col_next(1))
    near_b = send(near_a, col_next(1))

    spread = pltpu.VMEM((2, 2) + SPREAD, jnp.bfloat16)
    sent = [
        pltpu.VMEM((8, LANES), jnp.int32),
        pltpu.SMEM((8, LANES), jnp.int32),
        pltpu.SemaphoreType.DMA(()),
    ]
    far, far_left = call(
        far_kernel, [VMEM] * 5, (sums(), spread_shape()), [spread, TOTAL, PRODUCT_TABLE, *sent], 0, "far_three"
    )(far_a, far_b, right, right_y, right_z)
    far = call(far_last_kernel, [VMEM] * 5, sums(), [TOTAL, PRODUCT_TABLE, *sent], 10**9, "far_last")(
        far_a, far_left, right_0, right_1, far
    )
    received = send(far, z_far)
    near = call(near_kernel, [SMEM] * 4 + [VMEM] * 7, sums(), [spread, TOTAL, PRODUCT_TABLE], 3 * 10**9, "near_all")(
        *lists, near_a, near_b, right, right_y, right_z, right_0, right_1
    )
    return near + received


def shifted(shard, axis, by):
    devices = lax.axis_size(axis)
    return lax.ppermute(shard, axis, [(i, (i + by) % devices) for i in range(devices)])


def windowed(left, right, lists):
    cols = lax.axis_size("col")
    half_row, parity = lax.axis_index("row") // 2, lax.axis_index("row") % 2
    column = lax.axis_index("col")
    bits = cols.bit_length() - 1
    for bit in range(bits):
        right = jnp.where(column // (1 << bit) % 2 == 1, shifted(right, "row", -(2 << bit)), right)
        left = jnp.where(half_row // (1 << bit) % 2 == 1, shifted(left, "col", -(1 << bit)), left)
    total = jnp.zeros(SUMS, jnp.float32)
    for section in range(SECTIONS):
        swap = [(i, i ^ 1) for i in range(lax.axis_size("row"))]
        partner = lax.ppermute(right, "row", swap)
        kernel = functools.partial(pair_kernel, section=section)
        total = call(kernel, [SMEM] * 4 + [VMEM] * 4, sums(), [TOTAL, PRODUCT_TABLE], 2 * 10**9, "panel_pair")(
            *lists, left,
            jnp.where(parity == 0, right, partner), jnp.where(parity == 0, partner, right), total,
        )
        if section + 1 < SECTIONS:
            right = shifted(right, "row", -2)
            left = shifted(left, "col", -1)
    return total


def per_device(left_blocks, right_blocks, left_slots, right_slots, sink_slots, live_counts):
    left = left_view(left_blocks[0])
    right = right_blocks.reshape(RIGHT_SLOTS, HALF, LANES)
    lists = (left_slots[0, 0], right_slots[0, 0], sink_slots[0, 0], live_counts[0, 0])
    plan = grouped if lax.axis_size("col") == SECTIONS == 4 else windowed
    return plan(left, right, lists).reshape(1, 1, SINK_SLOTS, TILE_SIDE * TILE_SIDE)


def solution(mesh):
    return jax.shard_map(
        per_device,
        mesh=mesh,
        in_specs=(
            P("row", "col", None, None),
            P("row", "col", None, None),
            P("row", "col", None, None, None),
            P("row", "col", None, None, None),
            P("row", "col", None, None, None),
            P("row", "col", None, None),
        ),
        out_specs=P("row", "col", None, None),
        check_vma=False,
    )
```

```python
import functools

import jax
import jax.numpy as jnp
from jax import lax
from jax.experimental import pallas as pl
from jax.experimental.pallas import tpu as pltpu
from jax.sharding import PartitionSpec as P

TILE_SIDE = 64
LEFT_SLOTS = 4
RIGHT_SLOTS = 20
SINK_SLOTS = 12
PRODUCTS = 24
SECTIONS = 4
HALF = TILE_SIDE // 2
LANES = 2 * TILE_SIDE
LEFT_ROWS = 2 * LEFT_SLOTS * HALF
LIST_ROWS = 32
ODD_SINKS = 16
AXES = ("row", "col")
MIB = 1 << 20


def in_low_half(shape):
    return lax.broadcasted_iota(jnp.int32, shape, 1) % LANES < TILE_SIDE


def spread_table():
    shape = (2 * LANES, 8 * TILE_SIDE)
    source = lax.broadcasted_iota(jnp.int32, shape, 0)
    target = lax.broadcasted_iota(jnp.int32, shape, 1)
    place = target % TILE_SIDE
    part = target // TILE_SIDE % 2
    odd_row = target // (4 * TILE_SIDE)
    inner = 2 * (place % HALF) + place // HALF
    return (source == part * LANES + odd_row * TILE_SIDE + inner).astype(jnp.bfloat16)


def spread_left(blocks, table):
    high = blocks.astype(jnp.bfloat16)
    low = (blocks - high.astype(jnp.float32)).astype(jnp.bfloat16)
    both = jnp.concatenate([high, low], axis=1)
    wide = jnp.dot(both, table, preferred_element_type=jnp.float32).astype(jnp.bfloat16)
    return jnp.concatenate([wide[:, : 4 * TILE_SIDE], wide[:, 4 * TILE_SIDE :]], axis=0)


def slots_in_order(panel_ref, half):
    first = half * LEFT_SLOTS * HALF
    return jnp.concatenate(
        [panel_ref[pl.ds(first + slot, HALF, stride=LEFT_SLOTS), :] for slot in range(LEFT_SLOTS)], axis=0
    )


def in_parts(rows):
    high = rows.astype(jnp.bfloat16)
    low = (rows - high.astype(jnp.float32)).astype(jnp.bfloat16)
    return jnp.concatenate([high, high, low, low], axis=0)


def right_pair(first, second):
    low_half = in_low_half((HALF, LANES))
    first_turned = pltpu.roll(first, TILE_SIDE, 1)
    second_turned = pltpu.roll(second, TILE_SIDE, 1)
    one = [jnp.where(low_half, first, second_turned), jnp.where(low_half, first_turned, second)]
    other = [jnp.where(low_half, second, first_turned), jnp.where(low_half, second_turned, first)]
    return in_parts(jnp.concatenate(one, axis=0)), in_parts(jnp.concatenate(other, axis=0))


def all_products(left, right_ref, product_ref):
    rows = LEFT_SLOTS * HALF
    low_half = in_low_half((HALF, LANES))
    for slot in range(0, RIGHT_SLOTS, 4):
        pairs = [right_pair(right_ref[slot + n], right_ref[slot + n + 1]) for n in (0, 2)]
        even, odd = (
            jnp.dot(part, jnp.concatenate(tables, axis=1), preferred_element_type=jnp.float32)
            for part, tables in zip((left[:rows], left[rows:]), zip(*pairs))
        )
        for l in range(LEFT_SLOTS):
            for n in (0, 2):
                where = (slice(l * HALF, (l + 1) * HALF), slice(n * TILE_SIDE, (n + 2) * TILE_SIDE))
                place = l * RIGHT_SLOTS + slot + n
                product_ref[place] = jnp.where(low_half, even[where], odd[where])
                product_ref[place + 1] = jnp.where(low_half, odd[where], even[where])


def start_total(total_ref, before=None):
    total_ref[...] = jnp.zeros_like(total_ref)
    if before is not None:
        total_ref[:SINK_SLOTS] = before[...]


def whole_total(total_ref):
    turned = total_ref[ODD_SINKS : ODD_SINKS + SINK_SLOTS].reshape(SINK_SLOTS * HALF, LANES)
    return total_ref[:SINK_SLOTS] + pltpu.roll(turned, TILE_SIDE, 1).reshape(SUMS)


def add_listed(total_ref, product_ref, lists, section, half):
    for p in range(PRODUCTS):
        product, sink = lists.entry(section, half, p)
        total_ref[sink] += product_ref[product]


class OwnLists:
    def __init__(self, refs):
        self.refs = refs

    def entry(self, section, half, p):
        left, right, sink = (ref[section, half, p] for ref in self.refs[:3])
        live = self.refs[3][section, half]
        return left * RIGHT_SLOTS + right, right % 2 * ODD_SINKS + jnp.where(p < live, sink, SINK_SLOTS)


class SentLists:
    def __init__(self, panel_ref, whole, numbers, semaphore):
        left, right, sink, live = (
            panel_ref[LEFT_ROWS + 8 * n : LEFT_ROWS + 8 * (n + 1), :].astype(jnp.int32) for n in range(4)
        )
        here = lax.broadcasted_iota(jnp.int32, left.shape, 1) < live
        sink = right % 2 * ODD_SINKS + jnp.where(here, sink, SINK_SLOTS)
        whole[...] = (left * RIGHT_SLOTS + right) * 2 * ODD_SINKS + sink
        copy = pltpu.make_async_copy(whole, numbers, semaphore)
        copy.start()
        copy.wait()
        self.numbers = numbers

    def entry(self, section, half, p):
        number = self.numbers[section * 2 + half, p]
        return number // (2 * ODD_SINKS), number % (2 * ODD_SINKS)


class Place:
    def __init__(self):
        self.cols = lax.axis_size("col")
        row, self.col = lax.axis_index("row"), lax.axis_index("col")
        self.pair, self.half = row // 2, row % 2
        self.inside = self.col // 2 == self.pair // 2

    def which_left(self, level):
        return (self.pair + self.col + level) % 2

    def section(self, level, far):
        target = self.pair ^ 3 if far else self.pair
        return ((self.pair ^ level) - target - self.col + 2 * self.cols) % self.cols


def stage_kernel(left, left_list, right_list, sink_list, counts, left_out, rows_out, semaphore):
    copy = pltpu.make_async_copy(left, left_out, semaphore)
    copy.start()
    rows_out[...] = jnp.zeros_like(rows_out)
    for n, ref in enumerate((left_list, right_list, sink_list)):
        for section in range(SECTIONS):
            start = 8 * n + 2 * section
            rows_out[start : start + 2, :PRODUCTS] = ref[section].astype(jnp.float32)
    live = counts[...].astype(jnp.float32)
    for section in range(SECTIONS):
        for half in range(2):
            row = 24 + 2 * section + half
            one = live[section : section + 1, half : half + 1]
            rows_out[row : row + 1, :] = jnp.broadcast_to(one, (1, LANES))
    copy.wait()


def pick_kernel(left, beside, rows, near_out, far_out):
    inside = Place().inside

    @pl.when(inside)
    def _():
        near_out[...] = left[...]
        far_out[:LEFT_ROWS, :] = beside[...]

    @pl.when(jnp.logical_not(inside))
    def _():
        near_out[...] = beside[...]
        far_out[:LEFT_ROWS, :] = left[...]

    far_out[LEFT_ROWS:, :] = rows[...]


def spread_panels(lefts, panels):
    table = spread_table()
    for which, panel in enumerate(panels):
        for half in range(2):
            lefts[which, half] = spread_left(slots_in_order(panel, half), table)


def add_panels(panels, product_ref, total_ref, lists, lefts, place, far):
    for blocks, level, half in panels:
        all_products(lefts[place.which_left(level), half], blocks, product_ref)
        add_listed(total_ref, product_ref, lists, place.section(level, far), half)


def far_kernel(
    left_a, left_b, own, right_y, right_z,
    out, left_out, lefts, total, products, whole, numbers, semaphore,
):
    lists = SentLists(left_a, whole, numbers, semaphore)
    place = Place()
    half = place.half
    spread_panels(lefts, (left_a, left_b))
    left_out[...] = lefts[place.which_left(1), 1 - half]
    start_total(total)
    panels = ((own, 0, half), (right_y, 0, 1 - half), (right_z, 1, half))
    add_panels(panels, products, total, lists, lefts, place, True)
    out[...] = whole_total(total)


def far_last_kernel(
    left_a, left, right_d, before, out, total, products, whole, numbers, semaphore
):
    lists = SentLists(left_a, whole, numbers, semaphore)
    place = Place()
    start_total(total, before)
    all_products(left[...], right_d, products)
    add_listed(total, products, lists, place.section(1, True), 1 - place.half)
    out[...] = whole_total(total)


def near_kernel(
    l, r, s, n, left_a, left_b, own, right_y, right_z, right_d, out, lefts, total, products
):
    place = Place()
    half = place.half
    spread_panels(lefts, (left_a, left_b))
    start_total(total)
    panels = (
        (own, 0, half), (right_y, 0, 1 - half), (right_z, 1, half), (right_d, 1, 1 - half),
    )
    add_panels(panels, products, total, OwnLists((l, r, s, n)), lefts, place, False)
    out[...] = whole_total(total)


def pair_kernel(l, r, s, n, left, right_0, right_1, before, out, total, products, *, section):
    table = spread_table()
    start_total(total, before)
    for half, right in ((0, right_0), (1, right_1)):
        all_products(spread_left(slots_in_order(left, half), table), right, products)
        add_listed(total, products, OwnLists((l, r, s, n)), section, half)
    out[...] = whole_total(total)


STAGE_COST = 0
PICK_COST = 0
ANY = pl.BlockSpec(memory_space=pl.ANY)
SMEM = pl.BlockSpec(memory_space=pltpu.SMEM)
VMEM = pl.BlockSpec(memory_space=pltpu.VMEM)
SUMS = (SINK_SLOTS, HALF, LANES)
TOTAL = pltpu.VMEM((2 * ODD_SINKS, HALF, LANES), jnp.float32)
PRODUCT_TABLE = pltpu.VMEM((LEFT_SLOTS * RIGHT_SLOTS, HALF, LANES), jnp.float32)
SPREAD = (2 * LEFT_SLOTS * HALF, 4 * TILE_SIDE)


def call(kernel, specs, outs, scratch, flops, name):
    return pl.pallas_call(
        kernel,
        out_shape=outs,
        in_specs=specs,
        out_specs=jax.tree.map(lambda _: VMEM, outs),
        scratch_shapes=scratch,
        compiler_params=pltpu.CompilerParams(vmem_limit_bytes=24 * MIB),
        cost_estimate=pl.CostEstimate(flops=flops, bytes_accessed=0, transcendentals=0),
        name=name,
    )


def sums():
    return jax.ShapeDtypeStruct(SUMS, jnp.float32)


def left_panel(more):
    return jax.ShapeDtypeStruct((LEFT_ROWS + more, LANES), jnp.float32)


def spread_shape():
    return jax.ShapeDtypeStruct(SPREAD, jnp.bfloat16)


def left_view(panels):
    return panels.reshape(2, LEFT_SLOTS, HALF, LANES).transpose(0, 2, 1, 3).reshape(LEFT_ROWS, LANES)


def grouped(left, right, lists):
    cols = lax.axis_size("col")

    def device(pair, parity, col):
        return (2 * pair + parity) * cols + col

    def send(value, to):
        where = [
            (device(pair, parity, col), device(*to(pair, parity, col)))
            for pair in range(cols)
            for parity in range(2)
            for col in range(cols)
        ]
        return lax.ppermute(value, AXES, where)

    def y_next(pair, parity, col):
        return (pair, 1 - parity, col)

    def z_next(pair, parity, col):
        return (pair ^ 1, parity, col)

    def z_far(pair, parity, col):
        return (pair ^ 3, parity, col)

    def col_next(flip):
        return lambda pair, parity, col: (pair, parity, col ^ flip)

    beside = send(left, col_next(2))
    right_y = send(right, y_next)
    right_z = send(right, z_next)
    own_left, list_rows = call(
        stage_kernel, [ANY] + [VMEM] * 4, (left_panel(0), jax.ShapeDtypeStruct((LIST_ROWS, LANES), jnp.float32)),
        [pltpu.SemaphoreType.DMA(())], STAGE_COST, "stage",
    )(left, *lists)
    near_a, far_a = call(
        pick_kernel, [VMEM] * 3, (left_panel(0), left_panel(LIST_ROWS)), [], PICK_COST, "pick"
    )(own_left, beside, list_rows)
    far_a = send(far_a, z_far)
    right_d = send(right_z, y_next)
    far_b = send(far_a, col_next(1))
    near_b = send(near_a, col_next(1))

    spread = pltpu.VMEM((2, 2) + SPREAD, jnp.bfloat16)
    sent = [
        pltpu.VMEM((8, LANES), jnp.int32),
        pltpu.SMEM((8, LANES), jnp.int32),
        pltpu.SemaphoreType.DMA(()),
    ]
    far, far_left = call(
        far_kernel, [VMEM] * 5, (sums(), spread_shape()), [spread, TOTAL, PRODUCT_TABLE, *sent], 10**9, "far_three"
    )(far_a, far_b, right, right_y, right_z)
    far = call(far_last_kernel, [VMEM] * 4, sums(), [TOTAL, PRODUCT_TABLE, *sent], 10**9, "far_last")(
        far_a, far_left, right_d, far
    )
    received = send(far, z_far)
    near = call(near_kernel, [SMEM] * 4 + [VMEM] * 6, sums(), [spread, TOTAL, PRODUCT_TABLE], 3 * 10**9, "near_all")(
        *lists, near_a, near_b, right, right_y, right_z, right_d
    )
    return near + received


def shifted(shard, axis, by):
    devices = lax.axis_size(axis)
    return lax.ppermute(shard, axis, [(i, (i + by) % devices) for i in range(devices)])


def windowed(left, right, lists):
    cols = lax.axis_size("col")
    half_row, parity = lax.axis_index("row") // 2, lax.axis_index("row") % 2
    column = lax.axis_index("col")
    bits = cols.bit_length() - 1
    for bit in range(bits):
        right = jnp.where(column // (1 << bit) % 2 == 1, shifted(right, "row", -(2 << bit)), right)
        left = jnp.where(half_row // (1 << bit) % 2 == 1, shifted(left, "col", -(1 << bit)), left)
    total = jnp.zeros(SUMS, jnp.float32)
    for section in range(SECTIONS):
        swap = [(i, i ^ 1) for i in range(lax.axis_size("row"))]
        partner = lax.ppermute(right, "row", swap)
        kernel = functools.partial(pair_kernel, section=section)
        total = call(kernel, [SMEM] * 4 + [VMEM] * 4, sums(), [TOTAL, PRODUCT_TABLE], 2 * 10**9, "panel_pair")(
            *lists, left,
            jnp.where(parity == 0, right, partner), jnp.where(parity == 0, partner, right), total,
        )
        if section + 1 < SECTIONS:
            right = shifted(right, "row", -2)
            left = shifted(left, "col", -1)
    return total


def per_device(left_blocks, right_blocks, left_slots, right_slots, sink_slots, live_counts):
    left = left_view(left_blocks[0])
    right = right_blocks.reshape(RIGHT_SLOTS, HALF, LANES)
    lists = (left_slots[0, 0], right_slots[0, 0], sink_slots[0, 0], live_counts[0, 0])
    plan = grouped if lax.axis_size("col") == SECTIONS == 4 else windowed
    return plan(left, right, lists).reshape(1, 1, SINK_SLOTS, TILE_SIDE * TILE_SIDE)


def solution(mesh):
    return jax.shard_map(
        per_device,
        mesh=mesh,
        in_specs=(
            P("row", "col", None, None),
            P("row", "col", None, None),
            P("row", "col", None, None, None),
            P("row", "col", None, None, None),
            P("row", "col", None, None, None),
            P("row", "col", None, None),
        ),
        out_specs=P("row", "col", None, None),
        check_vma=False,
    )
```

```python
import functools

import jax
import jax.numpy as jnp
from jax import lax
from jax.experimental import pallas as pl
from jax.experimental.pallas import tpu as pltpu
from jax.sharding import PartitionSpec as P

TILE_SIDE = 64
LEFT_SLOTS = 4
RIGHT_SLOTS = 20
SINK_SLOTS = 12
PRODUCTS = 24
SECTIONS = 4
HALF = TILE_SIDE // 2
LANES = 2 * TILE_SIDE
LEFT_ROWS = 2 * LEFT_SLOTS * HALF
LIST_ROWS = 2 * SECTIONS
LIST_LANES = LANES // 4
ODD_SINKS = 16
AXES = ("row", "col")
MIB = 1 << 20


def in_low_half(shape):
    return lax.broadcasted_iota(jnp.int32, shape, 1) % LANES < TILE_SIDE


def spread_table():
    shape = (2 * LANES, 8 * TILE_SIDE)
    source = lax.broadcasted_iota(jnp.int32, shape, 0)
    target = lax.broadcasted_iota(jnp.int32, shape, 1)
    place = target % TILE_SIDE
    part = target // TILE_SIDE % 2
    odd_row = target // (4 * TILE_SIDE)
    inner = 2 * (place % HALF) + place // HALF
    return (source == part * LANES + odd_row * TILE_SIDE + inner).astype(jnp.bfloat16)


def spread_left(blocks, table):
    high = blocks.astype(jnp.bfloat16)
    low = (blocks - high.astype(jnp.float32)).astype(jnp.bfloat16)
    both = jnp.concatenate([high, low], axis=1)
    wide = jnp.dot(both, table, preferred_element_type=jnp.float32).astype(jnp.bfloat16)
    return jnp.concatenate([wide[:, : 4 * TILE_SIDE], wide[:, 4 * TILE_SIDE :]], axis=0)


def slots_in_order(panel_ref, half):
    first = half * LEFT_SLOTS * HALF
    return jnp.concatenate(
        [panel_ref[pl.ds(first + slot, HALF, stride=LEFT_SLOTS), :] for slot in range(LEFT_SLOTS)], axis=0
    )


def in_parts(rows):
    high = rows.astype(jnp.bfloat16)
    low = (rows - high.astype(jnp.float32)).astype(jnp.bfloat16)
    return jnp.concatenate([high, high, low, low], axis=0)


def right_pair(first, second):
    low_half = in_low_half((HALF, LANES))
    first_turned = pltpu.roll(first, TILE_SIDE, 1)
    second_turned = pltpu.roll(second, TILE_SIDE, 1)
    one = [jnp.where(low_half, first, second_turned), jnp.where(low_half, first_turned, second)]
    other = [jnp.where(low_half, second, first_turned), jnp.where(low_half, second_turned, first)]
    return in_parts(jnp.concatenate(one, axis=0)), in_parts(jnp.concatenate(other, axis=0))


def all_products(left, right_ref, product_ref):
    rows = LEFT_SLOTS * HALF
    low_half = in_low_half((HALF, LANES))
    for slot in range(0, RIGHT_SLOTS, 4):
        pairs = [right_pair(right_ref[slot + n], right_ref[slot + n + 1]) for n in (0, 2)]
        even, odd = (
            jnp.dot(part, jnp.concatenate(tables, axis=1), preferred_element_type=jnp.float32)
            for part, tables in zip((left[:rows], left[rows:]), zip(*pairs))
        )
        for l in range(LEFT_SLOTS):
            for n in (0, 2):
                where = (slice(l * HALF, (l + 1) * HALF), slice(n * TILE_SIDE, (n + 2) * TILE_SIDE))
                place = l * RIGHT_SLOTS + slot + n
                product_ref[place] = jnp.where(low_half, even[where], odd[where])
                product_ref[place + 1] = jnp.where(low_half, odd[where], even[where])


def start_total(total_ref, before=None):
    total_ref[...] = jnp.zeros_like(total_ref)
    if before is not None:
        total_ref[:SINK_SLOTS] = before[...]


def whole_total(total_ref):
    turned = total_ref[ODD_SINKS : ODD_SINKS + SINK_SLOTS].reshape(SINK_SLOTS * HALF, LANES)
    return total_ref[:SINK_SLOTS] + pltpu.roll(turned, TILE_SIDE, 1).reshape(SUMS)


def add_listed(total_ref, product_ref, lists, section, half):
    for p in range(PRODUCTS):
        product, sink = lists.entry(section, half, p)
        total_ref[sink] += product_ref[product]


class OwnLists:
    def __init__(self, refs):
        self.refs = refs

    def entry(self, section, half, p):
        left, right, sink = (ref[section, half, p] for ref in self.refs[:3])
        live = self.refs[3][section, half]
        return left * RIGHT_SLOTS + right, right % 2 * ODD_SINKS + jnp.where(p < live, sink, SINK_SLOTS)


class SentLists:
    def __init__(self, numbers):
        self.numbers = numbers

    def entry(self, section, half, p):
        number = self.numbers[section * 2 + half, p]
        return number // (2 * ODD_SINKS), number % (2 * ODD_SINKS)


def merge_kernel(panel_ref, numbers, whole, semaphore):
    rows = panel_ref[LEFT_ROWS:, :].astype(jnp.int32)
    left, right, sink, live = (pltpu.roll(rows, LANES - n * LIST_LANES, 1) if n else rows for n in range(4))
    here = lax.broadcasted_iota(jnp.int32, left.shape, 1) < live
    sink = right % 2 * ODD_SINKS + jnp.where(here, sink, SINK_SLOTS)
    whole[...] = (left * RIGHT_SLOTS + right) * 2 * ODD_SINKS + sink
    copy = pltpu.make_async_copy(whole, numbers, semaphore)
    copy.start()
    copy.wait()


class Place:
    def __init__(self):
        self.cols = lax.axis_size("col")
        row, self.col = lax.axis_index("row"), lax.axis_index("col")
        self.pair, self.half = row // 2, row % 2
        self.inside = self.col // 2 == self.pair // 2

    def which_left(self, level):
        return (self.pair + self.col + level) % 2

    def section(self, level, far):
        target = self.pair ^ 3 if far else self.pair
        return ((self.pair ^ level) - target - self.col + 2 * self.cols) % self.cols


def stage_kernel(left, left_list, right_list, sink_list, counts, left_out, rows_out, semaphore):
    copy = pltpu.make_async_copy(left, left_out, semaphore)
    copy.start()
    rows_out[...] = jnp.zeros_like(rows_out)
    live = counts[...].astype(jnp.float32)
    for section in range(SECTIONS):
        rows = slice(2 * section, 2 * section + 2)
        for n, ref in enumerate((left_list, right_list, sink_list)):
            rows_out[rows, n * LIST_LANES : n * LIST_LANES + PRODUCTS] = ref[section].astype(jnp.float32)
        for half in range(2):
            one = live[section : section + 1, half : half + 1]
            row = 2 * section + half
            rows_out[row : row + 1, 3 * LIST_LANES :] = jnp.broadcast_to(one, (1, LIST_LANES))
    copy.wait()


def pick_kernel(left, beside, rows, near_out, far_out):
    inside = Place().inside

    @pl.when(inside)
    def _():
        near_out[...] = left[...]
        far_out[:LEFT_ROWS, :] = beside[...]

    @pl.when(jnp.logical_not(inside))
    def _():
        near_out[...] = beside[...]
        far_out[:LEFT_ROWS, :] = left[...]

    far_out[LEFT_ROWS:, :] = rows[...]


def spread_panels(lefts, panels):
    table = spread_table()
    for which, panel in enumerate(panels):
        for half in range(2):
            lefts[which, half] = spread_left(slots_in_order(panel, half), table)


def add_panels(panels, product_ref, total_ref, lists, lefts, place, far):
    for blocks, level, half in panels:
        all_products(lefts[place.which_left(level), half], blocks, product_ref)
        add_listed(total_ref, product_ref, lists, place.section(level, far), half)


def far_kernel(
    numbers, left_a, left_b, own, right_y, right_z, out, left_out, lefts, total, products
):
    lists = SentLists(numbers)
    place = Place()
    half = place.half
    spread_panels(lefts, (left_a, left_b))
    left_out[...] = lefts[place.which_left(1), 1 - half]
    start_total(total)
    panels = ((own, 0, half), (right_y, 0, 1 - half), (right_z, 1, half))
    add_panels(panels, products, total, lists, lefts, place, True)
    out[...] = whole_total(total)


def far_last_kernel(
    numbers, left, right_d, before, out, total, products
):
    lists = SentLists(numbers)
    place = Place()
    start_total(total, before)
    all_products(left[...], right_d, products)
    add_listed(total, products, lists, place.section(1, True), 1 - place.half)
    out[...] = whole_total(total)


def near_kernel(
    l, r, s, n, left_a, left_b, own, right_y, right_z, right_d, out, lefts, total, products
):
    place = Place()
    half = place.half
    spread_panels(lefts, (left_a, left_b))
    start_total(total)
    panels = (
        (own, 0, half), (right_y, 0, 1 - half), (right_z, 1, half), (right_d, 1, 1 - half),
    )
    add_panels(panels, products, total, OwnLists((l, r, s, n)), lefts, place, False)
    out[...] = whole_total(total)


def pair_kernel(l, r, s, n, left, right_0, right_1, before, out, total, products, *, section):
    table = spread_table()
    start_total(total, before)
    for half, right in ((0, right_0), (1, right_1)):
        all_products(spread_left(slots_in_order(left, half), table), right, products)
        add_listed(total, products, OwnLists((l, r, s, n)), section, half)
    out[...] = whole_total(total)


STAGE_COST = 0
PICK_COST = 0
ANY = pl.BlockSpec(memory_space=pl.ANY)
SMEM = pl.BlockSpec(memory_space=pltpu.SMEM)
VMEM = pl.BlockSpec(memory_space=pltpu.VMEM)
SUMS = (SINK_SLOTS, HALF, LANES)
TOTAL = pltpu.VMEM((2 * ODD_SINKS, HALF, LANES), jnp.float32)
PRODUCT_TABLE = pltpu.VMEM((LEFT_SLOTS * RIGHT_SLOTS, HALF, LANES), jnp.float32)
SPREAD = (2 * LEFT_SLOTS * HALF, 4 * TILE_SIDE)


def call(kernel, specs, outs, scratch, flops, name):
    return pl.pallas_call(
        kernel,
        out_shape=outs,
        in_specs=specs,
        out_specs=jax.tree.map(lambda out: SMEM if out.dtype == jnp.int32 else VMEM, outs),
        scratch_shapes=scratch,
        compiler_params=pltpu.CompilerParams(vmem_limit_bytes=24 * MIB),
        cost_estimate=pl.CostEstimate(flops=flops, bytes_accessed=0, transcendentals=0),
        name=name,
    )


def sums():
    return jax.ShapeDtypeStruct(SUMS, jnp.float32)


def left_panel(more):
    return jax.ShapeDtypeStruct((LEFT_ROWS + more, LANES), jnp.float32)


def spread_shape():
    return jax.ShapeDtypeStruct(SPREAD, jnp.bfloat16)


def left_view(panels):
    return panels.reshape(2, LEFT_SLOTS, HALF, LANES).transpose(0, 2, 1, 3).reshape(LEFT_ROWS, LANES)


def grouped(left, right, lists):
    cols = lax.axis_size("col")

    def device(pair, parity, col):
        return (2 * pair + parity) * cols + col

    def send(value, to):
        where = [
            (device(pair, parity, col), device(*to(pair, parity, col)))
            for pair in range(cols)
            for parity in range(2)
            for col in range(cols)
        ]
        return lax.ppermute(value, AXES, where)

    def y_next(pair, parity, col):
        return (pair, 1 - parity, col)

    def z_next(pair, parity, col):
        return (pair ^ 1, parity, col)

    def z_far(pair, parity, col):
        return (pair ^ 3, parity, col)

    def col_next(flip):
        return lambda pair, parity, col: (pair, parity, col ^ flip)

    beside = send(left, col_next(2))
    right_y = send(right, y_next)
    right_z = send(right, z_next)
    own_left, list_rows = call(
        stage_kernel, [ANY] + [VMEM] * 4, (left_panel(0), jax.ShapeDtypeStruct((LIST_ROWS, LANES), jnp.float32)),
        [pltpu.SemaphoreType.DMA(())], STAGE_COST, "stage",
    )(left, *lists)
    near_a, far_a = call(
        pick_kernel, [VMEM] * 3, (left_panel(0), left_panel(LIST_ROWS)), [], PICK_COST, "pick"
    )(own_left, beside, list_rows)
    far_a = send(far_a, z_far)
    right_d = send(right_z, y_next)
    far_b = send(far_a, col_next(1))
    near_b = send(near_a, col_next(1))

    spread = pltpu.VMEM((2, 2) + SPREAD, jnp.bfloat16)
    numbers = call(
        merge_kernel, [VMEM], pltpu.SMEM((2 * SECTIONS, LANES), jnp.int32),
        [pltpu.VMEM((2 * SECTIONS, LANES), jnp.int32), pltpu.SemaphoreType.DMA(())], 0, "merge",
    )(far_a)
    far, far_left = call(
        far_kernel, [SMEM] + [VMEM] * 5, (sums(), spread_shape()), [spread, TOTAL, PRODUCT_TABLE], 10**9, "far_three"
    )(numbers, far_a, far_b, right, right_y, right_z)
    far = call(far_last_kernel, [SMEM] + [VMEM] * 3, sums(), [TOTAL, PRODUCT_TABLE], 10**9, "far_last")(
        numbers, far_left, right_d, far
    )
    received = send(far, z_far)
    near = call(near_kernel, [SMEM] * 4 + [VMEM] * 6, sums(), [spread, TOTAL, PRODUCT_TABLE], 3 * 10**9, "near_all")(
        *lists, near_a, near_b, right, right_y, right_z, right_d
    )
    return near + received


def shifted(shard, axis, by):
    devices = lax.axis_size(axis)
    return lax.ppermute(shard, axis, [(i, (i + by) % devices) for i in range(devices)])


def windowed(left, right, lists):
    cols = lax.axis_size("col")
    half_row, parity = lax.axis_index("row") // 2, lax.axis_index("row") % 2
    column = lax.axis_index("col")
    bits = cols.bit_length() - 1
    for bit in range(bits):
        right = jnp.where(column // (1 << bit) % 2 == 1, shifted(right, "row", -(2 << bit)), right)
        left = jnp.where(half_row // (1 << bit) % 2 == 1, shifted(left, "col", -(1 << bit)), left)
    total = jnp.zeros(SUMS, jnp.float32)
    for section in range(SECTIONS):
        swap = [(i, i ^ 1) for i in range(lax.axis_size("row"))]
        partner = lax.ppermute(right, "row", swap)
        kernel = functools.partial(pair_kernel, section=section)
        total = call(kernel, [SMEM] * 4 + [VMEM] * 4, sums(), [TOTAL, PRODUCT_TABLE], 2 * 10**9, "panel_pair")(
            *lists, left,
            jnp.where(parity == 0, right, partner), jnp.where(parity == 0, partner, right), total,
        )
        if section + 1 < SECTIONS:
            right = shifted(right, "row", -2)
            left = shifted(left, "col", -1)
    return total


def per_device(left_blocks, right_blocks, left_slots, right_slots, sink_slots, live_counts):
    left = left_view(left_blocks[0])
    right = right_blocks.reshape(RIGHT_SLOTS, HALF, LANES)
    lists = (left_slots[0, 0], right_slots[0, 0], sink_slots[0, 0], live_counts[0, 0])
    plan = grouped if lax.axis_size("col") == SECTIONS == 4 else windowed
    return plan(left, right, lists).reshape(1, 1, SINK_SLOTS, TILE_SIDE * TILE_SIDE)


def solution(mesh):
    return jax.shard_map(
        per_device,
        mesh=mesh,
        in_specs=(
            P("row", "col", None, None),
            P("row", "col", None, None),
            P("row", "col", None, None, None),
            P("row", "col", None, None, None),
            P("row", "col", None, None, None),
            P("row", "col", None, None),
        ),
        out_specs=P("row", "col", None, None),
        check_vma=False,
    )
```

```python
import functools

import jax
import jax.numpy as jnp
from jax import lax
from jax.experimental import pallas as pl
from jax.experimental.pallas import tpu as pltpu
from jax.sharding import PartitionSpec as P

TILE_SIDE = 64
LEFT_SLOTS = 4
RIGHT_SLOTS = 20
SINK_SLOTS = 12
PRODUCTS = 24
SECTIONS = 4
HALF = TILE_SIDE // 2
LANES = 2 * TILE_SIDE
LEFT_ROWS = 2 * LEFT_SLOTS * HALF
LIST_ROWS = 2 * SECTIONS
LIST_LANES = LANES // 4
SINK_BITS = 5
ODD_SINKS = 1 << (SINK_BITS - 1)
AXES = ("row", "col")
MIB = 1 << 20


def in_low_half(shape):
    return lax.broadcasted_iota(jnp.int32, shape, 1) % LANES < TILE_SIDE


def spread_table():
    shape = (2 * LANES, 8 * TILE_SIDE)
    source = lax.broadcasted_iota(jnp.int32, shape, 0)
    target = lax.broadcasted_iota(jnp.int32, shape, 1)
    place = target % TILE_SIDE
    part = target // TILE_SIDE % 2
    odd_row = target // (4 * TILE_SIDE)
    inner = 2 * (place % HALF) + place // HALF
    return (source == part * LANES + odd_row * TILE_SIDE + inner).astype(jnp.bfloat16)


def spread_left(blocks, table):
    high = blocks.astype(jnp.bfloat16)
    low = (blocks - high.astype(jnp.float32)).astype(jnp.bfloat16)
    both = jnp.concatenate([high, low], axis=1)
    wide = jnp.dot(both, table, preferred_element_type=jnp.float32).astype(jnp.bfloat16)
    return jnp.concatenate([wide[:, : 4 * TILE_SIDE], wide[:, 4 * TILE_SIDE :]], axis=0)


def slots_in_order(panel_ref, half):
    first = half * LEFT_SLOTS * HALF
    return jnp.concatenate(
        [panel_ref[pl.ds(first + slot, HALF, stride=LEFT_SLOTS), :] for slot in range(LEFT_SLOTS)], axis=0
    )


def in_parts(rows):
    high = rows.astype(jnp.bfloat16)
    low = (rows - high.astype(jnp.float32)).astype(jnp.bfloat16)
    return jnp.concatenate([high, high, low, low], axis=0)


def right_pair(first, second):
    low_half = in_low_half((HALF, LANES))
    first_turned = pltpu.roll(first, TILE_SIDE, 1)
    second_turned = pltpu.roll(second, TILE_SIDE, 1)
    one = [jnp.where(low_half, first, second_turned), jnp.where(low_half, first_turned, second)]
    other = [jnp.where(low_half, second, first_turned), jnp.where(low_half, second_turned, first)]
    return in_parts(jnp.concatenate(one, axis=0)), in_parts(jnp.concatenate(other, axis=0))


def all_products(left, right_ref, product_ref):
    rows = LEFT_SLOTS * HALF
    low_half = in_low_half((HALF, LANES))
    for slot in range(0, RIGHT_SLOTS, 4):
        pairs = [right_pair(right_ref[slot + n], right_ref[slot + n + 1]) for n in (0, 2)]
        even, odd = (
            jnp.dot(part, jnp.concatenate(tables, axis=1), preferred_element_type=jnp.float32)
            for part, tables in zip((left[:rows], left[rows:]), zip(*pairs))
        )
        for l in range(LEFT_SLOTS):
            for n in (0, 2):
                where = (slice(l * HALF, (l + 1) * HALF), slice(n * TILE_SIDE, (n + 2) * TILE_SIDE))
                place = l * RIGHT_SLOTS + slot + n
                product_ref[place] = jnp.where(low_half, even[where], odd[where])
                product_ref[place + 1] = jnp.where(low_half, odd[where], even[where])


def start_total(total_ref, before=None):
    total_ref[...] = jnp.zeros_like(total_ref)
    if before is not None:
        total_ref[:SINK_SLOTS] = before[...]


def whole_total(total_ref):
    turned = total_ref[ODD_SINKS : ODD_SINKS + SINK_SLOTS].reshape(SINK_SLOTS * HALF, LANES)
    return total_ref[:SINK_SLOTS] + pltpu.roll(turned, TILE_SIDE, 1).reshape(SUMS)


def add_listed(total_ref, product_ref, lists, section, half):
    for p in range(PRODUCTS):
        product, sink = lists.entry(section, half, p)
        total_ref[sink] += product_ref[product]


class OwnLists:
    def __init__(self, refs):
        self.refs = refs

    def entry(self, section, half, p):
        left, right, sink = (ref[section, half, p] for ref in self.refs[:3])
        live = self.refs[3][section, half]
        odd = (right & 1) * ODD_SINKS
        return left * RIGHT_SLOTS + right, odd + jnp.where(p < live, sink, SINK_SLOTS)


class SentLists:
    def __init__(self, numbers):
        self.numbers = numbers

    def entry(self, section, half, p):
        number = self.numbers[section * 2 + half, p]
        return number >> SINK_BITS, number & (2 * ODD_SINKS - 1)


def merge_kernel(panel_ref, numbers, whole, semaphore):
    rows = panel_ref[LEFT_ROWS:, :].astype(jnp.int32)
    left, right, sink, live = (pltpu.roll(rows, LANES - n * LIST_LANES, 1) if n else rows for n in range(4))
    here = lax.broadcasted_iota(jnp.int32, left.shape, 1) < live
    sink = right % 2 * ODD_SINKS + jnp.where(here, sink, SINK_SLOTS)
    product = jnp.where(here, left * RIGHT_SLOTS + right, 0)
    whole[...] = product * 2 * ODD_SINKS + sink
    copy = pltpu.make_async_copy(whole, numbers, semaphore)
    copy.start()
    copy.wait()


class Place:
    def __init__(self):
        self.cols = lax.axis_size("col")
        row, self.col = lax.axis_index("row"), lax.axis_index("col")
        self.pair, self.half = row // 2, row % 2
        self.inside = self.col // 2 == self.pair // 2

    def which_left(self, level):
        return (self.pair + self.col + level) % 2

    def section(self, level, far):
        target = self.pair ^ 3 if far else self.pair
        return ((self.pair ^ level) - target - self.col + 2 * self.cols) % self.cols


def stage_kernel(left, left_list, right_list, sink_list, counts, left_out, rows_out, semaphore):
    copy = pltpu.make_async_copy(left, left_out, semaphore)
    copy.start()
    rows_out[...] = jnp.zeros_like(rows_out)
    live = counts[...].astype(jnp.float32)
    for section in range(SECTIONS):
        rows = slice(2 * section, 2 * section + 2)
        for n, ref in enumerate((left_list, right_list, sink_list)):
            rows_out[rows, n * LIST_LANES : n * LIST_LANES + PRODUCTS] = ref[section].astype(jnp.float32)
        for half in range(2):
            one = live[section : section + 1, half : half + 1]
            row = 2 * section + half
            rows_out[row : row + 1, 3 * LIST_LANES :] = jnp.broadcast_to(one, (1, LIST_LANES))
    copy.wait()


def pick_kernel(left, beside, rows, near_out, far_out):
    inside = Place().inside

    @pl.when(inside)
    def _():
        near_out[...] = left[...]
        far_out[:LEFT_ROWS, :] = beside[...]

    @pl.when(jnp.logical_not(inside))
    def _():
        near_out[...] = beside[...]
        far_out[:LEFT_ROWS, :] = left[...]

    far_out[LEFT_ROWS:, :] = rows[...]


def spread_panels(lefts, panels):
    table = spread_table()
    for which, panel in enumerate(panels):
        for half in range(2):
            lefts[which, half] = spread_left(slots_in_order(panel, half), table)


def add_panels(panels, product_ref, total_ref, lists, lefts, place, far):
    for blocks, level, half in panels:
        all_products(lefts[place.which_left(level), half], blocks, product_ref)
        add_listed(total_ref, product_ref, lists, place.section(level, far), half)


def far_kernel(
    numbers, left_a, left_b, own, right_y, right_z, out, left_out, lefts, total, products
):
    lists = SentLists(numbers)
    place = Place()
    half = place.half
    spread_panels(lefts, (left_a, left_b))
    left_out[...] = lefts[place.which_left(1), 1 - half]
    start_total(total)
    panels = ((own, 0, half), (right_y, 0, 1 - half), (right_z, 1, half))
    add_panels(panels, products, total, lists, lefts, place, True)
    out[...] = whole_total(total)


def far_last_kernel(
    numbers, left, right_d, before, out, total, products
):
    lists = SentLists(numbers)
    place = Place()
    start_total(total, before)
    all_products(left[...], right_d, products)
    add_listed(total, products, lists, place.section(1, True), 1 - place.half)
    out[...] = whole_total(total)


def near_kernel(
    l, r, s, n, left_a, left_b, own, right_y, right_z, right_d, out, lefts, total, products
):
    place = Place()
    half = place.half
    spread_panels(lefts, (left_a, left_b))
    start_total(total)
    panels = (
        (own, 0, half), (right_y, 0, 1 - half), (right_z, 1, half), (right_d, 1, 1 - half),
    )
    add_panels(panels, products, total, OwnLists((l, r, s, n)), lefts, place, False)
    out[...] = whole_total(total)


def pair_kernel(l, r, s, n, left, right_0, right_1, before, out, total, products, *, section):
    table = spread_table()
    start_total(total, before)
    for half, right in ((0, right_0), (1, right_1)):
        all_products(spread_left(slots_in_order(left, half), table), right, products)
        add_listed(total, products, OwnLists((l, r, s, n)), section, half)
    out[...] = whole_total(total)


STAGE_COST = 0
PICK_COST = 0
ANY = pl.BlockSpec(memory_space=pl.ANY)
SMEM = pl.BlockSpec(memory_space=pltpu.SMEM)
VMEM = pl.BlockSpec(memory_space=pltpu.VMEM)
SUMS = (SINK_SLOTS, HALF, LANES)
TOTAL = pltpu.VMEM((2 * ODD_SINKS, HALF, LANES), jnp.float32)
PRODUCT_TABLE = pltpu.VMEM((LEFT_SLOTS * RIGHT_SLOTS, HALF, LANES), jnp.float32)
SPREAD = (2 * LEFT_SLOTS * HALF, 4 * TILE_SIDE)


def call(kernel, specs, outs, scratch, flops, name):
    return pl.pallas_call(
        kernel,
        out_shape=outs,
        in_specs=specs,
        out_specs=jax.tree.map(lambda out: SMEM if out.dtype == jnp.int32 else VMEM, outs),
        scratch_shapes=scratch,
        compiler_params=pltpu.CompilerParams(vmem_limit_bytes=24 * MIB),
        cost_estimate=pl.CostEstimate(flops=flops, bytes_accessed=0, transcendentals=0),
        name=name,
    )


def sums():
    return jax.ShapeDtypeStruct(SUMS, jnp.float32)


def left_panel(more):
    return jax.ShapeDtypeStruct((LEFT_ROWS + more, LANES), jnp.float32)


def spread_shape():
    return jax.ShapeDtypeStruct(SPREAD, jnp.bfloat16)


def left_view(panels):
    return panels.reshape(2, LEFT_SLOTS, HALF, LANES).transpose(0, 2, 1, 3).reshape(LEFT_ROWS, LANES)


def grouped(left, right, lists):
    cols = lax.axis_size("col")

    def device(pair, parity, col):
        return (2 * pair + parity) * cols + col

    def send(value, to):
        where = [
            (device(pair, parity, col), device(*to(pair, parity, col)))
            for pair in range(cols)
            for parity in range(2)
            for col in range(cols)
        ]
        return lax.ppermute(value, AXES, where)

    def y_next(pair, parity, col):
        return (pair, 1 - parity, col)

    def z_next(pair, parity, col):
        return (pair ^ 1, parity, col)

    def z_far(pair, parity, col):
        return (pair ^ 3, parity, col)

    def col_next(flip):
        return lambda pair, parity, col: (pair, parity, col ^ flip)

    beside = send(left, col_next(2))
    right_y = send(right, y_next)
    right_z = send(right, z_next)
    own_left, list_rows = call(
        stage_kernel, [ANY] + [VMEM] * 4, (left_panel(0), jax.ShapeDtypeStruct((LIST_ROWS, LANES), jnp.float32)),
        [pltpu.SemaphoreType.DMA(())], STAGE_COST, "stage",
    )(left, *lists)
    near_a, far_a = call(
        pick_kernel, [VMEM] * 3, (left_panel(0), left_panel(LIST_ROWS)), [], PICK_COST, "pick"
    )(own_left, beside, list_rows)
    far_a = send(far_a, z_far)
    right_d = send(right_z, y_next)
    far_b = send(far_a, col_next(1))
    near_b = send(near_a, col_next(1))

    spread = pltpu.VMEM((2, 2) + SPREAD, jnp.bfloat16)
    numbers = call(
        merge_kernel, [VMEM], pltpu.SMEM((2 * SECTIONS, LANES), jnp.int32),
        [pltpu.VMEM((2 * SECTIONS, LANES), jnp.int32), pltpu.SemaphoreType.DMA(())], 0, "merge",
    )(far_a)
    far, far_left = call(
        far_kernel, [SMEM] + [VMEM] * 5, (sums(), spread_shape()), [spread, TOTAL, PRODUCT_TABLE], 10**9, "far_three"
    )(numbers, far_a, far_b, right, right_y, right_z)
    far = call(far_last_kernel, [SMEM] + [VMEM] * 3, sums(), [TOTAL, PRODUCT_TABLE], 10**9, "far_last")(
        numbers, far_left, right_d, far
    )
    received = send(far, z_far)
    near = call(near_kernel, [SMEM] * 4 + [VMEM] * 6, sums(), [spread, TOTAL, PRODUCT_TABLE], 3 * 10**9, "near_all")(
        *lists, near_a, near_b, right, right_y, right_z, right_d
    )
    return near + received


def shifted(shard, axis, by):
    devices = lax.axis_size(axis)
    return lax.ppermute(shard, axis, [(i, (i + by) % devices) for i in range(devices)])


def windowed(left, right, lists):
    cols = lax.axis_size("col")
    half_row, parity = lax.axis_index("row") // 2, lax.axis_index("row") % 2
    column = lax.axis_index("col")
    bits = cols.bit_length() - 1
    for bit in range(bits):
        right = jnp.where(column // (1 << bit) % 2 == 1, shifted(right, "row", -(2 << bit)), right)
        left = jnp.where(half_row // (1 << bit) % 2 == 1, shifted(left, "col", -(1 << bit)), left)
    total = jnp.zeros(SUMS, jnp.float32)
    for section in range(SECTIONS):
        swap = [(i, i ^ 1) for i in range(lax.axis_size("row"))]
        partner = lax.ppermute(right, "row", swap)
        kernel = functools.partial(pair_kernel, section=section)
        total = call(kernel, [SMEM] * 4 + [VMEM] * 4, sums(), [TOTAL, PRODUCT_TABLE], 2 * 10**9, "panel_pair")(
            *lists, left,
            jnp.where(parity == 0, right, partner), jnp.where(parity == 0, partner, right), total,
        )
        if section + 1 < SECTIONS:
            right = shifted(right, "row", -2)
            left = shifted(left, "col", -1)
    return total


def per_device(left_blocks, right_blocks, left_slots, right_slots, sink_slots, live_counts):
    left = left_view(left_blocks[0])
    right = right_blocks.reshape(RIGHT_SLOTS, HALF, LANES)
    lists = (left_slots[0, 0], right_slots[0, 0], sink_slots[0, 0], live_counts[0, 0])
    plan = grouped if lax.axis_size("col") == SECTIONS == 4 else windowed
    return plan(left, right, lists).reshape(1, 1, SINK_SLOTS, TILE_SIDE * TILE_SIDE)


def solution(mesh):
    return jax.shard_map(
        per_device,
        mesh=mesh,
        in_specs=(
            P("row", "col", None, None),
            P("row", "col", None, None),
            P("row", "col", None, None, None),
            P("row", "col", None, None, None),
            P("row", "col", None, None, None),
            P("row", "col", None, None),
        ),
        out_specs=P("row", "col", None, None),
        check_vma=False,
    )
```

```python
import functools

import jax
import jax.numpy as jnp
from jax import lax
from jax.experimental import pallas as pl
from jax.experimental.pallas import tpu as pltpu
from jax.sharding import PartitionSpec as P

TILE_SIDE = 64
LEFT_SLOTS = 4
RIGHT_SLOTS = 20
SINK_SLOTS = 12
PRODUCTS = 24
SECTIONS = 4
HALF = TILE_SIDE // 2
LANES = 2 * TILE_SIDE
LEFT_ROWS = 2 * LEFT_SLOTS * HALF
LIST_ROWS = 2 * SECTIONS
LIST_LANES = LANES // 4
SINK_BITS = 5
ODD_SINKS = 1 << (SINK_BITS - 1)
AXES = ("row", "col")
MIB = 1 << 20


def in_low_half(shape):
    return lax.broadcasted_iota(jnp.int32, shape, 1) % LANES < TILE_SIDE


def spread_table():
    shape = (2 * LANES, 8 * TILE_SIDE)
    source = lax.broadcasted_iota(jnp.int32, shape, 0)
    target = lax.broadcasted_iota(jnp.int32, shape, 1)
    place = target % TILE_SIDE
    part = target // TILE_SIDE % 2
    odd_row = target // (4 * TILE_SIDE)
    inner = 2 * (place % HALF) + place // HALF
    return (source == part * LANES + odd_row * TILE_SIDE + inner).astype(jnp.bfloat16)


def spread_left(blocks, table):
    high = blocks.astype(jnp.bfloat16)
    low = (blocks - high.astype(jnp.float32)).astype(jnp.bfloat16)
    both = jnp.concatenate([high, low], axis=1)
    wide = jnp.dot(both, table, preferred_element_type=jnp.float32).astype(jnp.bfloat16)
    return jnp.concatenate([wide[:, : 4 * TILE_SIDE], wide[:, 4 * TILE_SIDE :]], axis=0)


def slots_in_order(panel_ref, half):
    first = half * LEFT_SLOTS * HALF
    return jnp.concatenate(
        [panel_ref[pl.ds(first + slot, HALF, stride=LEFT_SLOTS), :] for slot in range(LEFT_SLOTS)], axis=0
    )


def in_parts(rows):
    high = rows.astype(jnp.bfloat16)
    low = (rows - high.astype(jnp.float32)).astype(jnp.bfloat16)
    return jnp.concatenate([high, high, low, low], axis=0)


def right_pair(first, second):
    low_half = in_low_half((HALF, LANES))
    first_turned = pltpu.roll(first, TILE_SIDE, 1)
    second_turned = pltpu.roll(second, TILE_SIDE, 1)
    one = [jnp.where(low_half, first, second_turned), jnp.where(low_half, first_turned, second)]
    other = [jnp.where(low_half, second, first_turned), jnp.where(low_half, second_turned, first)]
    return in_parts(jnp.concatenate(one, axis=0)), in_parts(jnp.concatenate(other, axis=0))


def all_products(left, right_ref, product_ref):
    rows = LEFT_SLOTS * HALF
    low_half = in_low_half((HALF, LANES))
    for slot in range(0, RIGHT_SLOTS, 4):
        pairs = [right_pair(right_ref[slot + n], right_ref[slot + n + 1]) for n in (0, 2)]
        even, odd = (
            jnp.dot(part, jnp.concatenate(tables, axis=1), preferred_element_type=jnp.float32)
            for part, tables in zip((left[:rows], left[rows:]), zip(*pairs))
        )
        for l in range(LEFT_SLOTS):
            for n in (0, 2):
                where = (slice(l * HALF, (l + 1) * HALF), slice(n * TILE_SIDE, (n + 2) * TILE_SIDE))
                place = l * RIGHT_SLOTS + slot + n
                product_ref[place] = jnp.where(low_half, even[where], odd[where])
                product_ref[place + 1] = jnp.where(low_half, odd[where], even[where])


def start_total(total_ref, before=None):
    total_ref[...] = jnp.zeros_like(total_ref)
    if before is not None:
        total_ref[:SINK_SLOTS] = before[...]


def whole_total(total_ref):
    turned = total_ref[ODD_SINKS : ODD_SINKS + SINK_SLOTS].reshape(SINK_SLOTS * HALF, LANES)
    return total_ref[:SINK_SLOTS] + pltpu.roll(turned, TILE_SIDE, 1).reshape(SUMS)


def add_listed(total_ref, product_ref, lists, section, half):
    for p in range(PRODUCTS):
        product, sink = lists.entry(section, half, p)
        total_ref[sink] += product_ref[product]


class OwnLists:
    def __init__(self, refs):
        self.refs = refs

    def entry(self, section, half, p):
        left, right, sink = (ref[section, half, p] for ref in self.refs[:3])
        live = self.refs[3][section, half]
        odd = (right & 1) * ODD_SINKS
        return left * RIGHT_SLOTS + right, odd + jnp.where(p < live, sink, SINK_SLOTS)


class SentLists:
    def __init__(self, numbers):
        self.numbers = numbers

    def entry(self, section, half, p):
        number = self.numbers[section * 2 + half, p]
        return number >> SINK_BITS, number & (2 * ODD_SINKS - 1)


def merge_kernel(panel_ref, numbers, whole, semaphore):
    rows = panel_ref[LEFT_ROWS:, :].astype(jnp.int32)
    left, right, sink, live = (pltpu.roll(rows, LANES - n * LIST_LANES, 1) if n else rows for n in range(4))
    here = lax.broadcasted_iota(jnp.int32, left.shape, 1) < live
    sink = right % 2 * ODD_SINKS + jnp.where(here, sink, SINK_SLOTS)
    product = jnp.where(here, left * RIGHT_SLOTS + right, 0)
    whole[...] = product * 2 * ODD_SINKS + sink
    copy = pltpu.make_async_copy(whole, numbers, semaphore)
    copy.start()
    copy.wait()


class Place:
    def __init__(self):
        self.cols = lax.axis_size("col")
        row, self.col = lax.axis_index("row"), lax.axis_index("col")
        self.pair, self.half = row // 2, row % 2
        self.inside = self.col // 2 == self.pair // 2

    def which_left(self, level):
        return (self.pair + self.col + level) % 2

    def section(self, level, far):
        target = self.pair ^ 3 if far else self.pair
        return ((self.pair ^ level) - target - self.col + 2 * self.cols) % self.cols


def stage_kernel(left, left_list, right_list, sink_list, counts, left_out, rows_out, table_out, semaphore):
    copy = pltpu.make_async_copy(left, left_out, semaphore)
    copy.start()
    table_out[...] = spread_table()
    rows_out[...] = jnp.zeros_like(rows_out)
    live = counts[...].astype(jnp.float32)
    for section in range(SECTIONS):
        rows = slice(2 * section, 2 * section + 2)
        for n, ref in enumerate((left_list, right_list, sink_list)):
            rows_out[rows, n * LIST_LANES : n * LIST_LANES + PRODUCTS] = ref[section].astype(jnp.float32)
        for half in range(2):
            one = live[section : section + 1, half : half + 1]
            row = 2 * section + half
            rows_out[row : row + 1, 3 * LIST_LANES :] = jnp.broadcast_to(one, (1, LIST_LANES))
    copy.wait()


def pick_kernel(left, beside, rows, near_out, far_out):
    inside = Place().inside

    @pl.when(inside)
    def _():
        near_out[...] = left[...]
        far_out[:LEFT_ROWS, :] = beside[...]

    @pl.when(jnp.logical_not(inside))
    def _():
        near_out[...] = beside[...]
        far_out[:LEFT_ROWS, :] = left[...]

    far_out[LEFT_ROWS:, :] = rows[...]


def spread_panels(lefts, panels, table):
    for which, panel in enumerate(panels):
        for half in range(2):
            lefts[which, half] = spread_left(slots_in_order(panel, half), table)


def add_panels(panels, product_ref, total_ref, lists, lefts, place, far):
    for blocks, level, half in panels:
        all_products(lefts[place.which_left(level), half], blocks, product_ref)
        add_listed(total_ref, product_ref, lists, place.section(level, far), half)


def far_kernel(
    numbers, table, left_a, left_b, own, right_y, right_z, out, left_out, lefts, total, products
):
    lists = SentLists(numbers)
    place = Place()
    half = place.half
    spread_panels(lefts, (left_a, left_b), table[...])
    left_out[...] = lefts[place.which_left(1), 1 - half]
    start_total(total)
    panels = ((own, 0, half), (right_y, 0, 1 - half), (right_z, 1, half))
    add_panels(panels, products, total, lists, lefts, place, True)
    out[...] = whole_total(total)


def far_last_kernel(
    numbers, left, right_d, before, out, total, products
):
    lists = SentLists(numbers)
    place = Place()
    start_total(total)
    all_products(left[...], right_d, products)
    add_listed(total, products, lists, place.section(1, True), 1 - place.half)
    out[...] = before[...] + whole_total(total)


def near_kernel(
    l, r, s, n, table, left_a, left_b, own, right_y, right_z, right_d, out, lefts, total, products
):
    place = Place()
    half = place.half
    spread_panels(lefts, (left_a, left_b), table[...])
    start_total(total)
    panels = (
        (own, 0, half), (right_y, 0, 1 - half), (right_z, 1, half), (right_d, 1, 1 - half),
    )
    add_panels(panels, products, total, OwnLists((l, r, s, n)), lefts, place, False)
    out[...] = whole_total(total)


def pair_kernel(l, r, s, n, left, right_0, right_1, before, out, total, products, *, section):
    table = spread_table()
    start_total(total, before)
    for half, right in ((0, right_0), (1, right_1)):
        all_products(spread_left(slots_in_order(left, half), table), right, products)
        add_listed(total, products, OwnLists((l, r, s, n)), section, half)
    out[...] = whole_total(total)


STAGE_COST = 0
PICK_COST = 0
ANY = pl.BlockSpec(memory_space=pl.ANY)
SMEM = pl.BlockSpec(memory_space=pltpu.SMEM)
VMEM = pl.BlockSpec(memory_space=pltpu.VMEM)
SUMS = (SINK_SLOTS, HALF, LANES)
TOTAL = pltpu.VMEM((2 * ODD_SINKS, HALF, LANES), jnp.float32)
PRODUCT_TABLE = pltpu.VMEM((LEFT_SLOTS * RIGHT_SLOTS, HALF, LANES), jnp.float32)
SPREAD = (2 * LEFT_SLOTS * HALF, 4 * TILE_SIDE)


def call(kernel, specs, outs, scratch, flops, name):
    return pl.pallas_call(
        kernel,
        out_shape=outs,
        in_specs=specs,
        out_specs=jax.tree.map(lambda out: SMEM if out.dtype == jnp.int32 else VMEM, outs),
        scratch_shapes=scratch,
        compiler_params=pltpu.CompilerParams(vmem_limit_bytes=24 * MIB),
        cost_estimate=pl.CostEstimate(flops=flops, bytes_accessed=0, transcendentals=0),
        name=name,
    )


def sums():
    return jax.ShapeDtypeStruct(SUMS, jnp.float32)


def left_panel(more):
    return jax.ShapeDtypeStruct((LEFT_ROWS + more, LANES), jnp.float32)


def spread_shape():
    return jax.ShapeDtypeStruct(SPREAD, jnp.bfloat16)


def left_view(panels):
    return panels.reshape(2, LEFT_SLOTS, HALF, LANES).transpose(0, 2, 1, 3).reshape(LEFT_ROWS, LANES)


def grouped(left, right, lists):
    cols = lax.axis_size("col")

    def device(pair, parity, col):
        return (2 * pair + parity) * cols + col

    def send(value, to):
        where = [
            (device(pair, parity, col), device(*to(pair, parity, col)))
            for pair in range(cols)
            for parity in range(2)
            for col in range(cols)
        ]
        return lax.ppermute(value, AXES, where)

    def y_next(pair, parity, col):
        return (pair, 1 - parity, col)

    def z_next(pair, parity, col):
        return (pair ^ 1, parity, col)

    def z_far(pair, parity, col):
        return (pair ^ 3, parity, col)

    def col_next(flip):
        return lambda pair, parity, col: (pair, parity, col ^ flip)

    beside = send(left, col_next(2))
    right_y = send(right, y_next)
    right_z = send(right, z_next)
    own_left, list_rows, table = call(
        stage_kernel, [ANY] + [VMEM] * 4, (left_panel(0), jax.ShapeDtypeStruct((LIST_ROWS, LANES), jnp.float32),
         jax.ShapeDtypeStruct((2 * LANES, 8 * TILE_SIDE), jnp.bfloat16)),
        [pltpu.SemaphoreType.DMA(())], STAGE_COST, "stage",
    )(left, *lists)
    near_a, far_a = call(
        pick_kernel, [VMEM] * 3, (left_panel(0), left_panel(LIST_ROWS)), [], PICK_COST, "pick"
    )(own_left, beside, list_rows)
    far_a = send(far_a, z_far)
    right_d = send(right_z, y_next)
    far_b = send(far_a, col_next(1))
    near_b = send(near_a, col_next(1))

    spread = pltpu.VMEM((2, 2) + SPREAD, jnp.bfloat16)
    numbers = call(
        merge_kernel, [VMEM], pltpu.SMEM((2 * SECTIONS, LANES), jnp.int32),
        [pltpu.VMEM((2 * SECTIONS, LANES), jnp.int32), pltpu.SemaphoreType.DMA(())], 0, "merge",
    )(far_a)
    far, far_left = call(
        far_kernel, [SMEM] + [VMEM] * 6, (sums(), spread_shape()), [spread, TOTAL, PRODUCT_TABLE], 10**9, "far_three"
    )(numbers, table, far_a, far_b, right, right_y, right_z)
    far = call(far_last_kernel, [SMEM] + [VMEM] * 3, sums(), [TOTAL, PRODUCT_TABLE], 0, "far_last")(
        numbers, far_left, right_d, far
    )
    received = send(far, z_far)
    near = call(near_kernel, [SMEM] * 4 + [VMEM] * 7, sums(), [spread, TOTAL, PRODUCT_TABLE], 3 * 10**9, "near_all")(
        *lists, table, near_a, near_b, right, right_y, right_z, right_d
    )
    return near + received


def shifted(shard, axis, by):
    devices = lax.axis_size(axis)
    return lax.ppermute(shard, axis, [(i, (i + by) % devices) for i in range(devices)])


def windowed(left, right, lists):
    cols = lax.axis_size("col")
    half_row, parity = lax.axis_index("row") // 2, lax.axis_index("row") % 2
    column = lax.axis_index("col")
    bits = cols.bit_length() - 1
    for bit in range(bits):
        right = jnp.where(column // (1 << bit) % 2 == 1, shifted(right, "row", -(2 << bit)), right)
        left = jnp.where(half_row // (1 << bit) % 2 == 1, shifted(left, "col", -(1 << bit)), left)
    total = jnp.zeros(SUMS, jnp.float32)
    for section in range(SECTIONS):
        swap = [(i, i ^ 1) for i in range(lax.axis_size("row"))]
        partner = lax.ppermute(right, "row", swap)
        kernel = functools.partial(pair_kernel, section=section)
        total = call(kernel, [SMEM] * 4 + [VMEM] * 4, sums(), [TOTAL, PRODUCT_TABLE], 2 * 10**9, "panel_pair")(
            *lists, left,
            jnp.where(parity == 0, right, partner), jnp.where(parity == 0, partner, right), total,
        )
        if section + 1 < SECTIONS:
            right = shifted(right, "row", -2)
            left = shifted(left, "col", -1)
    return total


def per_device(left_blocks, right_blocks, left_slots, right_slots, sink_slots, live_counts):
    left = left_view(left_blocks[0])
    right = right_blocks.reshape(RIGHT_SLOTS, HALF, LANES)
    lists = (left_slots[0, 0], right_slots[0, 0], sink_slots[0, 0], live_counts[0, 0])
    plan = grouped if lax.axis_size("col") == SECTIONS == 4 else windowed
    return plan(left, right, lists).reshape(1, 1, SINK_SLOTS, TILE_SIDE * TILE_SIDE)


def solution(mesh):
    return jax.shard_map(
        per_device,
        mesh=mesh,
        in_specs=(
            P("row", "col", None, None),
            P("row", "col", None, None),
            P("row", "col", None, None, None),
            P("row", "col", None, None, None),
            P("row", "col", None, None, None),
            P("row", "col", None, None),
        ),
        out_specs=P("row", "col", None, None),
        check_vma=False,
    )
```

```python
import functools

import jax
import jax.numpy as jnp
from jax import lax
from jax.experimental import pallas as pl
from jax.experimental.pallas import tpu as pltpu
from jax.sharding import PartitionSpec as P

TILE_SIDE = 64
LEFT_SLOTS = 4
RIGHT_SLOTS = 20
SINK_SLOTS = 12
PRODUCTS = 24
SECTIONS = 4
HALF = TILE_SIDE // 2
LANES = 2 * TILE_SIDE
LEFT_ROWS = 2 * LEFT_SLOTS * HALF
LIST_ROWS = 2 * SECTIONS
LIST_LANES = LANES // 4
SINK_BITS = 5
ODD_SINKS = 1 << (SINK_BITS - 1)
AXES = ("row", "col")
MIB = 1 << 20


def in_low_half(shape):
    return lax.broadcasted_iota(jnp.int32, shape, 1) % LANES < TILE_SIDE


def spread_table():
    shape = (2 * LANES, 8 * TILE_SIDE)
    source = lax.broadcasted_iota(jnp.int32, shape, 0)
    target = lax.broadcasted_iota(jnp.int32, shape, 1)
    place = target % TILE_SIDE
    part = target // TILE_SIDE % 2
    odd_row = target // (4 * TILE_SIDE)
    inner = 2 * (place % HALF) + place // HALF
    return (source == part * LANES + odd_row * TILE_SIDE + inner).astype(jnp.bfloat16)


def spread_left(blocks, table):
    high = blocks.astype(jnp.bfloat16)
    low = (blocks - high.astype(jnp.float32)).astype(jnp.bfloat16)
    both = jnp.concatenate([high, low], axis=1)
    wide = jnp.dot(both, table, preferred_element_type=jnp.float32).astype(jnp.bfloat16)
    return jnp.concatenate([wide[:, : 4 * TILE_SIDE], wide[:, 4 * TILE_SIDE :]], axis=0)


def slots_in_order(panel_ref, half):
    first = half * LEFT_SLOTS * HALF
    return jnp.concatenate(
        [panel_ref[pl.ds(first + slot, HALF, stride=LEFT_SLOTS), :] for slot in range(LEFT_SLOTS)], axis=0
    )


def in_parts(rows):
    high = rows.astype(jnp.bfloat16)
    low = (rows - high.astype(jnp.float32)).astype(jnp.bfloat16)
    return jnp.concatenate([high, high, low, low], axis=0)


def right_pair(first, second):
    low_half = in_low_half((HALF, LANES))
    first_turned = pltpu.roll(first, TILE_SIDE, 1)
    second_turned = pltpu.roll(second, TILE_SIDE, 1)
    one = [jnp.where(low_half, first, second_turned), jnp.where(low_half, first_turned, second)]
    other = [jnp.where(low_half, second, first_turned), jnp.where(low_half, second_turned, first)]
    return in_parts(jnp.concatenate(one, axis=0)), in_parts(jnp.concatenate(other, axis=0))


def all_products(left, right_ref, product_ref):
    rows = LEFT_SLOTS * HALF
    low_half = in_low_half((HALF, LANES))
    for slot in range(0, RIGHT_SLOTS, 4):
        pairs = [right_pair(right_ref[slot + n], right_ref[slot + n + 1]) for n in (0, 2)]
        even, odd = (
            jnp.dot(part, jnp.concatenate(tables, axis=1), preferred_element_type=jnp.float32)
            for part, tables in zip((left[:rows], left[rows:]), zip(*pairs))
        )
        for l in range(LEFT_SLOTS):
            for n in (0, 2):
                where = (slice(l * HALF, (l + 1) * HALF), slice(n * TILE_SIDE, (n + 2) * TILE_SIDE))
                place = l * RIGHT_SLOTS + slot + n
                product_ref[place] = jnp.where(low_half, even[where], odd[where])
                product_ref[place + 1] = jnp.where(low_half, odd[where], even[where])


def start_total(total_ref, before=None):
    total_ref[...] = jnp.zeros_like(total_ref)
    if before is not None:
        total_ref[:SINK_SLOTS] = before[...]


def whole_total(total_ref):
    turned = total_ref[ODD_SINKS : ODD_SINKS + SINK_SLOTS].reshape(SINK_SLOTS * HALF, LANES)
    return total_ref[:SINK_SLOTS] + pltpu.roll(turned, TILE_SIDE, 1).reshape(SUMS)


def add_listed(total_ref, product_ref, lists, section, half):
    for p in range(PRODUCTS):
        product, sink = lists.entry(section, half, p)
        total_ref[sink] += product_ref[product]


class OwnLists:
    def __init__(self, refs):
        self.refs = refs

    def entry(self, section, half, p):
        left, right, sink = (ref[section, half, p] for ref in self.refs[:3])
        live = self.refs[3][section, half]
        return left * RIGHT_SLOTS + right, right % 2 * ODD_SINKS + jnp.where(p < live, sink, SINK_SLOTS)


class SentLists:
    def __init__(self, numbers):
        self.numbers = numbers

    def entry(self, section, half, p):
        number = self.numbers[section * 2 + half, p]
        return number >> SINK_BITS, number & (2 * ODD_SINKS - 1)


def merge_kernel(panel_ref, numbers, whole, semaphore):
    rows = panel_ref[LEFT_ROWS:, :].astype(jnp.int32)
    left, right, sink, live = (pltpu.roll(rows, LANES - n * LIST_LANES, 1) if n else rows for n in range(4))
    here = lax.broadcasted_iota(jnp.int32, left.shape, 1) < live
    sink = right % 2 * ODD_SINKS + jnp.where(here, sink, SINK_SLOTS)
    whole[...] = (left * RIGHT_SLOTS + right) * 2 * ODD_SINKS + sink
    copy = pltpu.make_async_copy(whole, numbers, semaphore)
    copy.start()
    copy.wait()


class Place:
    def __init__(self):
        self.cols = lax.axis_size("col")
        row, self.col = lax.axis_index("row"), lax.axis_index("col")
        self.pair, self.half = row // 2, row % 2
        self.inside = self.col // 2 == self.pair // 2

    def which_left(self, level):
        return (self.pair + self.col + level) % 2

    def section(self, level, far):
        target = self.pair ^ 3 if far else self.pair
        return ((self.pair ^ level) - target - self.col + 2 * self.cols) % self.cols


def stage_kernel(left, left_list, right_list, sink_list, counts, left_out, rows_out, semaphore):
    copy = pltpu.make_async_copy(left, left_out, semaphore)
    copy.start()
    rows_out[...] = jnp.zeros_like(rows_out)
    live = counts[...].astype(jnp.float32)
    for section in range(SECTIONS):
        rows = slice(2 * section, 2 * section + 2)
        for n, ref in enumerate((left_list, right_list, sink_list)):
            rows_out[rows, n * LIST_LANES : n * LIST_LANES + PRODUCTS] = ref[section].astype(jnp.float32)
        for half in range(2):
            one = live[section : section + 1, half : half + 1]
            row = 2 * section + half
            rows_out[row : row + 1, 3 * LIST_LANES :] = jnp.broadcast_to(one, (1, LIST_LANES))
    copy.wait()


def pick_kernel(left, beside, rows, near_out, far_out):
    inside = Place().inside

    @pl.when(inside)
    def _():
        near_out[...] = left[...]
        far_out[:LEFT_ROWS, :] = beside[...]

    @pl.when(jnp.logical_not(inside))
    def _():
        near_out[...] = beside[...]
        far_out[:LEFT_ROWS, :] = left[...]

    far_out[LEFT_ROWS:, :] = rows[...]


def spread_panels(lefts, panels):
    table = spread_table()
    for which, panel in enumerate(panels):
        for half in range(2):
            lefts[which, half] = spread_left(slots_in_order(panel, half), table)


def add_panels(panels, product_ref, total_ref, lists, lefts, place, far):
    for blocks, level, half in panels:
        all_products(lefts[place.which_left(level), half], blocks, product_ref)
        add_listed(total_ref, product_ref, lists, place.section(level, far), half)


def far_kernel(
    numbers, left_a, left_b, own, right_y, right_z, out, left_out, lefts, total, products
):
    lists = SentLists(numbers)
    place = Place()
    half = place.half
    spread_panels(lefts, (left_a, left_b))
    left_out[...] = lefts[place.which_left(1), 1 - half]
    start_total(total)
    panels = ((own, 0, half), (right_y, 0, 1 - half), (right_z, 1, half))
    add_panels(panels, products, total, lists, lefts, place, True)
    out[...] = whole_total(total)


def far_last_kernel(
    numbers, left, right_d, before, out, total, products
):
    lists = SentLists(numbers)
    place = Place()
    start_total(total)
    all_products(left[...], right_d, products)
    add_listed(total, products, lists, place.section(1, True), 1 - place.half)
    out[...] = before[...] + whole_total(total)


def near_kernel(
    l, r, s, n, left_a, left_b, own, right_y, right_z, right_d, out, lefts, total, products
):
    place = Place()
    half = place.half
    spread_panels(lefts, (left_a, left_b))
    start_total(total)
    panels = (
        (own, 0, half), (right_y, 0, 1 - half), (right_z, 1, half), (right_d, 1, 1 - half),
    )
    add_panels(panels, products, total, OwnLists((l, r, s, n)), lefts, place, False)
    out[...] = whole_total(total)


def pair_kernel(l, r, s, n, left, right_0, right_1, before, out, total, products, *, section):
    table = spread_table()
    start_total(total, before)
    for half, right in ((0, right_0), (1, right_1)):
        all_products(spread_left(slots_in_order(left, half), table), right, products)
        add_listed(total, products, OwnLists((l, r, s, n)), section, half)
    out[...] = whole_total(total)


STAGE_COST = 0
PICK_COST = 0
ANY = pl.BlockSpec(memory_space=pl.ANY)
SMEM = pl.BlockSpec(memory_space=pltpu.SMEM)
VMEM = pl.BlockSpec(memory_space=pltpu.VMEM)
SUMS = (SINK_SLOTS, HALF, LANES)
TOTAL = pltpu.VMEM((2 * ODD_SINKS, HALF, LANES), jnp.float32)
PRODUCT_TABLE = pltpu.VMEM((LEFT_SLOTS * RIGHT_SLOTS, HALF, LANES), jnp.float32)
SPREAD = (2 * LEFT_SLOTS * HALF, 4 * TILE_SIDE)


def call(kernel, specs, outs, scratch, flops, name):
    return pl.pallas_call(
        kernel,
        out_shape=outs,
        in_specs=specs,
        out_specs=jax.tree.map(lambda out: SMEM if out.dtype == jnp.int32 else VMEM, outs),
        scratch_shapes=scratch,
        compiler_params=pltpu.CompilerParams(vmem_limit_bytes=24 * MIB),
        cost_estimate=pl.CostEstimate(flops=flops, bytes_accessed=0, transcendentals=0),
        name=name,
    )


def sums():
    return jax.ShapeDtypeStruct(SUMS, jnp.float32)


def left_panel(more):
    return jax.ShapeDtypeStruct((LEFT_ROWS + more, LANES), jnp.float32)


def spread_shape():
    return jax.ShapeDtypeStruct(SPREAD, jnp.bfloat16)


def left_view(panels):
    return panels.reshape(2, LEFT_SLOTS, HALF, LANES).transpose(0, 2, 1, 3).reshape(LEFT_ROWS, LANES)


def grouped(left, right, lists):
    cols = lax.axis_size("col")

    def device(pair, parity, col):
        return (2 * pair + parity) * cols + col

    def send(value, to):
        where = [
            (device(pair, parity, col), device(*to(pair, parity, col)))
            for pair in range(cols)
            for parity in range(2)
            for col in range(cols)
        ]
        return lax.ppermute(value, AXES, where)

    def y_next(pair, parity, col):
        return (pair, 1 - parity, col)

    def z_next(pair, parity, col):
        return (pair ^ 1, parity, col)

    def z_far(pair, parity, col):
        return (pair ^ 3, parity, col)

    def col_next(flip):
        return lambda pair, parity, col: (pair, parity, col ^ flip)

    beside = send(left, col_next(2))
    right_y = send(right, y_next)
    right_z = send(right, z_next)
    own_left, list_rows = call(
        stage_kernel, [ANY] + [VMEM] * 4, (left_panel(0), jax.ShapeDtypeStruct((LIST_ROWS, LANES), jnp.float32)),
        [pltpu.SemaphoreType.DMA(())], STAGE_COST, "stage",
    )(left, *lists)
    near_a, far_a = call(
        pick_kernel, [VMEM] * 3, (left_panel(0), left_panel(LIST_ROWS)), [], PICK_COST, "pick"
    )(own_left, beside, list_rows)
    far_a = send(far_a, z_far)
    right_d = send(right_z, y_next)
    far_b = send(far_a, col_next(1))
    near_b = send(near_a, col_next(1))

    spread = pltpu.VMEM((2, 2) + SPREAD, jnp.bfloat16)
    numbers = call(
        merge_kernel, [VMEM], pltpu.SMEM((2 * SECTIONS, LANES), jnp.int32),
        [pltpu.VMEM((2 * SECTIONS, LANES), jnp.int32), pltpu.SemaphoreType.DMA(())], 0, "merge",
    )(far_a)
    far, far_left = call(
        far_kernel, [SMEM] + [VMEM] * 5, (sums(), spread_shape()), [spread, TOTAL, PRODUCT_TABLE], 10**9, "far_three"
    )(numbers, far_a, far_b, right, right_y, right_z)
    far = call(far_last_kernel, [SMEM] + [VMEM] * 3, sums(), [TOTAL, PRODUCT_TABLE], 10**9, "far_last")(
        numbers, far_left, right_d, far
    )
    received = send(far, z_far)
    near = call(near_kernel, [SMEM] * 4 + [VMEM] * 6, sums(), [spread, TOTAL, PRODUCT_TABLE], 3 * 10**9, "near_all")(
        *lists, near_a, near_b, right, right_y, right_z, right_d
    )
    return near + received


def shifted(shard, axis, by):
    devices = lax.axis_size(axis)
    return lax.ppermute(shard, axis, [(i, (i + by) % devices) for i in range(devices)])


def windowed(left, right, lists):
    cols = lax.axis_size("col")
    half_row, parity = lax.axis_index("row") // 2, lax.axis_index("row") % 2
    column = lax.axis_index("col")
    bits = cols.bit_length() - 1
    for bit in range(bits):
        right = jnp.where(column // (1 << bit) % 2 == 1, shifted(right, "row", -(2 << bit)), right)
        left = jnp.where(half_row // (1 << bit) % 2 == 1, shifted(left, "col", -(1 << bit)), left)
    total = jnp.zeros(SUMS, jnp.float32)
    for section in range(SECTIONS):
        swap = [(i, i ^ 1) for i in range(lax.axis_size("row"))]
        partner = lax.ppermute(right, "row", swap)
        kernel = functools.partial(pair_kernel, section=section)
        total = call(kernel, [SMEM] * 4 + [VMEM] * 4, sums(), [TOTAL, PRODUCT_TABLE], 2 * 10**9, "panel_pair")(
            *lists, left,
            jnp.where(parity == 0, right, partner), jnp.where(parity == 0, partner, right), total,
        )
        if section + 1 < SECTIONS:
            right = shifted(right, "row", -2)
            left = shifted(left, "col", -1)
    return total


def per_device(left_blocks, right_blocks, left_slots, right_slots, sink_slots, live_counts):
    left = left_view(left_blocks[0])
    right = right_blocks.reshape(RIGHT_SLOTS, HALF, LANES)
    lists = (left_slots[0, 0], right_slots[0, 0], sink_slots[0, 0], live_counts[0, 0])
    plan = grouped if lax.axis_size("col") == SECTIONS == 4 else windowed
    return plan(left, right, lists).reshape(1, 1, SINK_SLOTS, TILE_SIDE * TILE_SIDE)


def solution(mesh):
    return jax.shard_map(
        per_device,
        mesh=mesh,
        in_specs=(
            P("row", "col", None, None),
            P("row", "col", None, None),
            P("row", "col", None, None, None),
            P("row", "col", None, None, None),
            P("row", "col", None, None, None),
            P("row", "col", None, None),
        ),
        out_specs=P("row", "col", None, None),
        check_vma=False,
    )
```
